256 devices in a mesh: dp: 16 (over y_lo, x, core), feat: 16 (over z, y_hi).
Axes of the slice: x: 4, y: 4 (y_hi: 2, y_lo: 2; y = y_hi * 2 + y_lo), z: 8, core: 2. Of those that a mesh axis runs over, the one named last changes fastest.
Arguments:
- view_one: bfloat16 [3840, 8192], P('dp', 'feat'), may hold values from -25 to 25
- view_two: bfloat16 [3840, 8192], P('feat', 'dp'), may hold values from -25 to 25
- inputs_one: bfloat16 [3840, 8192], P(None, 'dp'), may hold values from -6 to 6
- inputs_two: bfloat16 [3840, 8192], P(None, 'feat'), may hold values from -6 to 6
- loss_scale: float32 [1], replicated, may hold values from 32 to 128
Outputs:
- loss_value: float32 [1], replicated
- weight_grad_one: float32 [8192, 8192], P('dp', 'feat')
- weight_grad_two: float32 [8192, 8192], P('feat', 'dp')
The draws below stay inside these ranges and needn't reach their ends.
All inputs are finite; a program needn't handle non-finite values.
Results may differ from the reference program's by a relative error of at most 0.0075.
Values may be sent and summed in bfloat16 or wider, within the bound.
A program may use at most 128 MiB of HBM per device.

```python
import math
import jax
import jax.numpy as jnp
from jax import lax

F = 8192
H = 8192
BATCH = 3840


def shared_signal(key):
    first, second, third = jax.random.split(key, 3)
    gauss = jnp.clip(jax.random.normal(first, (BATCH, F), jnp.float32), -5.0, 5.0)
    base = gauss
    scales = jnp.exp(jax.random.uniform(second, (F,), jnp.float32, math.log(0.5), math.log(4.0)))
    offsets = jax.random.uniform(third, (F,), jnp.float32, -2.0, 2.0)
    return base * scales + offsets


def draw_view_one(key, part):
    signal = shared_signal(key)
    key = jax.random.fold_in(key, 7)
    noise = 0.6 * jnp.clip(jax.random.normal(key, (BATCH, F), jnp.float32), -5.0, 5.0)
    return (signal + noise).astype(jnp.bfloat16)


def draw_view_two(key, part):
    signal = shared_signal(key)
    key = jax.random.fold_in(key, 13)
    noise = 0.6 * jnp.clip(jax.random.normal(key, (BATCH, F), jnp.float32), -5.0, 5.0)
    return (signal + noise).astype(jnp.bfloat16)


def block_levels(own_key, dims, pieces, smallest, top_value):
    def one(dim, parts):
        steps = jax.random.uniform(jax.random.fold_in(jax.random.fold_in(own_key, 6), dim), (parts,), jnp.float32, smallest / len(pieces), top_value / len(pieces))
        return jnp.repeat(jnp.exp(steps), dims[dim] // parts).reshape((-1,) + (1,) * (len(dims) - dim - 1))

    factor_of = one(*pieces[0])
    for cut in pieces[1:]:
        factor_of = factor_of * one(*cut)
    return factor_of


def scatter_about(key, dims, scale, bound, shards=(), kind=jnp.bfloat16):
    loudness = block_levels(key, dims, shards, -0.22, 0.18) if shards else 1.0
    array = jax.random.normal(key, dims, jnp.float32) * scale * loudness
    return jnp.minimum(jnp.maximum(array, -bound), bound).astype(kind)


def setup_inputs(seed: int = 0) -> dict:
    key_of = jax.random.split(jax.random.key(seed), 6)
    return {
        "view_one": draw_view_one(jax.random.fold_in(key_of[5], 71), 0),
        "view_two": draw_view_two(jax.random.fold_in(key_of[5], 71), 0),
        "inputs_one": scatter_about(key_of[2], (BATCH, H), 1.0, 6.0, ((1, 16),)),
        "inputs_two": scatter_about(key_of[3], (BATCH, H), 1.0, 6.0, ((1, 16),)),
        "loss_scale": jnp.clip(jnp.exp(jax.random.uniform(key_of[4], (1,), jnp.float32, math.log(32.0), math.log(128.0))), 32.0, 128.0),
    }


off_weight = 0.0051
epsilon = 1e-05

def column_moments(block):
    values = block.astype(jnp.float32)
    return (lax.optimization_barrier(jnp.sum(values, axis=0)), lax.optimization_barrier(jnp.sum(values * values, axis=0)))

def finish(sums, squares, batch_rows):
    average = sums / batch_rows
    spread = squares / batch_rows - average * average
    return (average, lax.rsqrt(spread + epsilon))

def standardize(block, average, inv_std):
    return ((block.astype(jnp.float32) - average) * inv_std).astype(jnp.bfloat16)

def apply_delta(upstream, normed, inv_std, first, second, batch_rows):
    own = normed.astype(jnp.float32)
    return (inv_std * (upstream - first / batch_rows - own * second / batch_rows)).astype(jnp.bfloat16)

def reference(view_one, view_two, inputs_one, inputs_two, loss_scale):
    batch_rows = view_one.shape[0]
    width = view_one.shape[1]
    sums_one, squares_one = column_moments(view_one)
    average_one, inv_one = finish(sums_one, squares_one, batch_rows)
    sums_two, squares_two = column_moments(view_two)
    average_two, inv_two = finish(sums_two, squares_two, batch_rows)
    normed_one = standardize(view_one, average_one, inv_one)
    normed_two = standardize(view_two, average_two, inv_two)
    block_size = math.gcd(width, 512)
    block_count = width // block_size
    scaling = loss_scale[0]

    def visit(carry, index):
        start = (index * block_size).astype(jnp.int32)
        rows_block = lax.dynamic_slice_in_dim(normed_one, start, block_size, 1)
        correlation = jnp.dot(rows_block.T, normed_two, preferred_element_type=jnp.float32) / batch_rows
        row_ids = start + lax.broadcasted_iota(jnp.int32, correlation.shape, 0)
        col_ids = lax.broadcasted_iota(jnp.int32, correlation.shape, 1)
        on_diagonal = row_ids == col_ids
        part_loss = jnp.sum(jnp.where(on_diagonal, (1.0 - correlation) * (1.0 - correlation), off_weight * correlation * correlation))
        gradient = (jnp.where(on_diagonal, -2.0 * (1.0 - correlation), 2.0 * off_weight * correlation) * scaling).astype(jnp.bfloat16)
        upward = jnp.dot(normed_two, gradient.T, preferred_element_type=jnp.float32)
        carry = carry + jnp.dot(rows_block, gradient, preferred_element_type=jnp.float32)
        return (carry, (part_loss, upward))
    initial = jnp.zeros((batch_rows, width), jnp.float32)
    summed, (losses, upwards) = lax.scan(visit, initial, jnp.arange(block_count, dtype=jnp.int32))
    upstream_one = jnp.transpose(upwards, (1, 0, 2)).reshape(batch_rows, width) / batch_rows
    upstream_two = summed / batch_rows
    first_one = lax.optimization_barrier(jnp.sum(upstream_one, axis=0))
    second_one = lax.optimization_barrier(jnp.sum(upstream_one * normed_one.astype(jnp.float32), axis=0))
    delta_one = apply_delta(upstream_one, normed_one, inv_one, first_one, second_one, batch_rows)
    first_two = lax.optimization_barrier(jnp.sum(upstream_two, axis=0))
    second_two = lax.optimization_barrier(jnp.sum(upstream_two * normed_two.astype(jnp.float32), axis=0))
    delta_two = apply_delta(upstream_two, normed_two, inv_two, first_two, second_two, batch_rows)
    weight_grad_one = jnp.dot(inputs_one.T, delta_one, preferred_element_type=jnp.float32)
    weight_grad_two = jnp.dot(inputs_two.T, delta_two, preferred_element_type=jnp.float32)
    loss_value = jnp.reshape(jnp.sum(losses) / width, (1,))
    return (loss_value, weight_grad_one, weight_grad_two)
```

```python
import jax
import jax.numpy as jnp
from jax import lax
from jax.experimental import pallas as pl
from jax.experimental.pallas import tpu as pltpu
from jax.sharding import PartitionSpec as P

F = 8192
off_weight = 0.0051
epsilon = 1e-05
MESH = pl.DeviceIdType.MESH
f32 = jnp.float32
bf16 = jnp.bfloat16

NX = 4
NZ = 8
SIGN = {"zp": 1, "zm": -1, "xp": 1, "xm": -1}
KZ = {("zp", 0): 4, ("zm", 0): 3, ("zp", 1): 3, ("zm", 1): 4}
KX = {("xp", 0): 2, ("xm", 0): 1, ("xp", 1): 1, ("xm", 1): 2}
ZSLOT = {}
for key, hops in KZ.items():
    for hop in range(hops):
        ZSLOT[key + (hop,)] = len(ZSLOT)
XSLOT = {}
for key, hops in KX.items():
    for hop in range(hops):
        XSLOT[key + (hop,)] = len(XSLOT)
CORDER = [(0, 2), (1, 2), (1, 1), (0, 3), (0, 1), (1, 3), (1, 0), (0, 0)]
CSLOT = {key: n for n, key in enumerate(CORDER)}
NSEM = 112


def dot_tn(left, right):
    return lax.dot_general(left, right, (((0,), (0,)), ((), ())), preferred_element_type=f32)


def dot_nt(left, right):
    return lax.dot_general(left, right, (((1,), (1,)), ((), ())), preferred_element_type=f32)


def dot_nn(left, right):
    return lax.dot_general(left, right, (((1,), (0,)), ((), ())), preferred_element_type=f32)


def fold8(block):
    total = block[0:8]
    for k in range(8, block.shape[0], 8):
        total = total + block[k : k + 8]
    return total


def kernel(
    view1, view2, in1, in2, scale_ref,
    loss_ref, w1_ref, w2_ref,
    V1, V2, D1, D2, X1, X2,
    zs, zr, cs, cr, xs, xr, ys, yr, U1, U2,
    C, G, GH, GL, M1, M2, A1, R1, A2, R2, AL, RL,
    ssem, rsem, lsem,
):
    R = view1.shape[0]
    B = V1.shape[0]
    T = V1.shape[1]
    dp = lax.axis_index("dp")
    ft = lax.axis_index("feat")
    c = lax.rem(dp, 2)
    x = lax.rem(lax.div(dp, 2), NX)
    yl = lax.div(dp, 2 * NX)
    yh = lax.rem(ft, 2)
    z = lax.div(ft, 2)

    def dpi(r, dx, other=0):
        y_ = yl if r == 0 else 1 - yl
        c_ = 1 - c if other else c
        return (y_ * NX + lax.rem(x + (dx % NX), NX)) * 2 + c_

    def fti(r, dz):
        y_ = yh if r == 0 else 1 - yh
        return lax.rem(z + (dz % NZ), NZ) * 2 + y_

    def rows(i):
        return pl.ds(pl.multiple_of(i * R, 16), R)

    def at(buf, i):
        return buf.at[rows(i)]

    to_core = {"dp": dpi(0, 0, 1), "feat": ft}
    to_yl = {"dp": dpi(1, 0), "feat": ft}
    to_yh = {"dp": dp, "feat": fti(1, 0)}
    to = {
        "xp": {"dp": dpi(0, 1), "feat": ft},
        "xm": {"dp": dpi(0, -1), "feat": ft},
        "zp": {"dp": dp, "feat": fti(0, 1)},
        "zm": {"dp": dp, "feat": fti(0, -1)},
    }
    xa = x + 1 - 2 * lax.rem(x, 2)
    xb = NX - 1 - x
    za = z + 1 - 2 * lax.rem(z, 2)
    zb = z + 2 - 4 * lax.rem(lax.div(z, 2), 2)
    dp_steps = [
        to_core,
        to_yl,
        {"dp": (yl * NX + xa) * 2 + c, "feat": ft},
        {"dp": (yl * NX + xb) * 2 + c, "feat": ft},
    ]
    to_zb = {"dp": dp, "feat": zb * 2 + yh}
    to_zc = {"dp": dp, "feat": fti(0, 4)}
    feat_steps = [to_yh, {"dp": dp, "feat": za * 2 + yh}, to_zb, to_zc]

    peers = [to_core, to_yl, to_yh, to["xp"], to["xm"], to["zp"], to["zm"], to_zb, to_zc]
    barrier = pltpu.get_barrier_semaphore()
    for peer in peers:
        pl.semaphore_signal(barrier, inc=1, device_id=peer, device_id_type=MESH)
    local = [
        pltpu.make_async_copy(view1, at(V1, dp), lsem.at[0]),
        pltpu.make_async_copy(view2, at(V2, ft), lsem.at[1]),
        pltpu.make_async_copy(in1, X1, lsem.at[2]),
        pltpu.make_async_copy(in2, X2, lsem.at[3]),
    ]
    for copy in local:
        copy.start()
    pl.semaphore_wait(barrier, len(peers))

    names = {}
    flying = {}

    def index(name):
        return names.setdefault(name, len(names))

    def send(name, src, dst, dev):
        k = index(name)
        copy = pltpu.make_async_remote_copy(
            src_ref=src, dst_ref=dst, send_sem=ssem.at[k], recv_sem=rsem.at[k],
            device_id=dev, device_id_type=MESH,
        )
        copy.start()
        flying[name] = copy

    def recv(name, dst):
        k = index(name)
        pltpu.make_async_remote_copy(
            src_ref=dst, dst_ref=dst, send_sem=ssem.at[k], recv_sem=rsem.at[k],
            device_id=to_core, device_id_type=MESH,
        ).wait_recv()

    def drain(keep=lambda name: True):
        for name in [n for n in flying if keep(n)]:
            flying.pop(name).wait_send()

    def start_a(tag, A, src):
        own = at(A, dp)
        send((tag, "yl"), src, own, to_yl)
        send((tag, "xp", 0, 1), src, own, to["xp"])
        send((tag, "xm", 0, 1), src, own, to["xm"])
        send((tag, "c", 0, 0), src, own, to_core)

    def start_b(tag, Bb, src):
        own = at(Bb, ft)
        send((tag, "yh"), src, own, to_yh)
        send((tag, "zp", 0, 1), src, own, to["zp"])
        send((tag, "zm", 0, 1), src, own, to["zm"])

    def ev_yl(tag, A):
        i = dpi(1, 0)
        recv((tag, "yl"), at(A, i))
        send((tag, "xp", 1, 1), at(A, i), at(A, i), to["xp"])
        send((tag, "xm", 1, 1), at(A, i), at(A, i), to["xm"])
        send((tag, "c", 1, 0), at(A, i), at(A, i), to_core)
        return i

    def ev_yh(tag, Bb):
        i = fti(1, 0)
        recv((tag, "yh"), at(Bb, i))
        send((tag, "zp", 1, 1), at(Bb, i), at(Bb, i), to["zp"])
        send((tag, "zm", 1, 1), at(Bb, i), at(Bb, i), to["zm"])
        return i

    def ev_x(tag, A, d, r, h):
        dx = (-SIGN[d] * h) % NX
        i = dpi(r, dx)
        recv((tag, d, r, h), at(A, i))
        if h < KX[d, r]:
            send((tag, d, r, h + 1), at(A, i), at(A, i), to[d])
        send((tag, "c", r, dx), at(A, i), at(A, i), to_core)
        return i

    def ev_z(tag, Bb, d, r, h):
        i = fti(r, -SIGN[d] * h)
        recv((tag, d, r, h), at(Bb, i))
        if h < KZ[d, r]:
            send((tag, d, r, h + 1), at(Bb, i), at(Bb, i), to[d])
        return i

    def ev_c(tag, A, r, dx):
        i = dpi(r, dx, 1)
        recv((tag, "c", r, dx), at(A, i))
        return i

    CH = 48

    def moments(V, M, i):
        base = i * R

        def body(k, carry):
            s, q = carry
            v = V[pl.ds(pl.multiple_of(base + k * CH, 16), CH), :].astype(f32)
            return s + fold8(v), q + fold8(v * v)

        s, q = lax.fori_loop(0, R // CH, body, (M[0:8, :], M[8:16, :]))
        M[0:8, :] = s
        M[8:16, :] = q

    def normalize(V, M):
        average = jnp.sum(M[0:8, :], axis=0, keepdims=True) / B
        spread = jnp.sum(M[8:16, :], axis=0, keepdims=True) / B - average * average
        inv = lax.rsqrt(spread + epsilon)
        M[16:24, :] = jnp.broadcast_to(inv, (8, T))

        def body(k, total):
            at_ = pl.ds(pl.multiple_of(k * CH, 16), CH)
            n = ((V[at_, :].astype(f32) - average) * inv).astype(bf16)
            V[at_, :] = n
            return total + fold8(n.astype(f32))

        total = lax.fori_loop(0, B // CH, body, jnp.zeros((8, T), f32))
        M[24:32, :] = jnp.broadcast_to(jnp.sum(total, axis=0, keepdims=True), (8, T))

    M1[...] = jnp.zeros_like(M1)
    M2[...] = jnp.zeros_like(M2)
    start_b("g", V2, view2)
    start_a("g", V1, view1)
    local[0].wait()
    local[1].wait()
    moments(V1, M1, dp)
    moments(V2, M2, ft)

    def gz(d, r, h):
        moments(V2, M2, ev_z("g", V2, d, r, h))

    def gx(d, r, h):
        moments(V1, M1, ev_x("g", V1, d, r, h))

    def gc(r, dx):
        moments(V1, M1, ev_c("g", V1, r, dx))

    gz("zp", 0, 1)
    gz("zm", 0, 1)
    moments(V1, M1, ev_yl("g", V1))
    gx("xp", 0, 1)
    gx("xm", 0, 1)
    moments(V2, M2, ev_yh("g", V2))
    gz("zp", 0, 2)
    gz("zm", 0, 2)
    gx("xp", 1, 1)
    gx("xm", 1, 1)
    gz("zp", 1, 1)
    gz("zm", 1, 1)
    gx("xp", 0, 2)
    gx("xm", 1, 2)
    gz("zp", 0, 3)
    gz("zm", 0, 3)
    gz("zp", 1, 2)
    gz("zm", 1, 2)
    for r, dx in CORDER:
        gc(r, dx)
    gz("zp", 0, 4)
    gz("zp", 1, 3)
    gz("zm", 1, 3)
    drain(lambda n: n[1] in ("c", "xp", "xm", "yl"))
    normalize(V1, M1)
    gz("zm", 1, 4)
    drain()
    normalize(V2, M2)

    KC = 768
    C[...] = dot_tn(V1[0:KC, :], V2[0:KC, :])

    def corr(k, carry):
        at_ = pl.ds(pl.multiple_of(k * KC, 16), KC)
        C[...] += dot_tn(V1[at_, :], V2[at_, :])
        return carry

    lax.fori_loop(1, B // KC, corr, 0)

    CG = 32
    scale = scale_ref[0]
    row0 = ft * T
    col0 = dp * T

    def grad(k, loss):
        at_ = pl.ds(pl.multiple_of(k * CG, CG), CG)
        corr_ = C[at_, :] / B
        row_ids = row0 + k * CG + lax.broadcasted_iota(jnp.int32, (CG, T), 0)
        col_ids = col0 + lax.broadcasted_iota(jnp.int32, (CG, T), 1)
        on = row_ids == col_ids
        miss = 1.0 - corr_
        loss = loss + fold8(jnp.where(on, miss * miss, off_weight * corr_ * corr_))
        g = (jnp.where(on, -2.0 * miss, 2.0 * off_weight * corr_) * scale).astype(bf16)
        G[at_, :] = g
        prod = g.astype(f32) * corr_
        high = prod.astype(bf16)
        GH[at_, :] = high
        GL[at_, :] = (prod - high.astype(f32)).astype(bf16)
        return loss

    loss = lax.fori_loop(0, T // CG, grad, jnp.zeros((8, T), f32))
    loss_tile = loss[:, 0:128]
    for k in range(128, T, 128):
        loss_tile = loss_tile + loss[:, k : k + 128]

    def p2(i):
        return dot_nn(V1[rows(i), :], G[...])

    def p1(i):
        return dot_nt(V2[rows(i), :], G[...])

    def zc(d, r, s):
        i = fti(r, SIGN[d] * (KZ[d, r] - s))
        val = p2(i)
        if s:
            prev = ZSLOT[d, r, s - 1]
            recv(("s", d, r, s - 1), zr.at[prev])
            val = val + zr[prev].astype(f32)
        slot = ZSLOT[d, r, s]
        zs[slot] = val.astype(bf16)
        send(("s", d, r, s), zs.at[slot], zr.at[slot], to[d])

    def z_end(r):
        val = p2(fti(r, 0))
        for d in ("zp", "zm"):
            last = KZ[d, r] - 1
            slot = ZSLOT[d, r, last]
            recv(("s", d, r, last), zr.at[slot])
            val = val + zr[slot].astype(f32)
        return val

    def core_send(r, dx):
        slot = CSLOT[r, dx]
        cs[slot] = p1(dpi(r, dx, 1)).astype(bf16)
        send(("s", "c", r, dx), cs.at[slot], cr.at[slot], to_core)

    def both(r, dx):
        dx = dx % NX
        val = p1(dpi(r, dx))
        slot = CSLOT[r, dx]
        recv(("s", "c", r, dx), cr.at[slot])
        return val + cr[slot].astype(f32)

    def xc(d, r, s):
        val = both(r, SIGN[d] * (KX[d, r] - s))
        if s:
            prev = XSLOT[d, r, s - 1]
            recv(("s", d, r, s - 1), xr.at[prev])
            val = val + xr[prev].astype(f32)
        slot = XSLOT[d, r, s]
        xs[slot] = val.astype(bf16)
        send(("s", d, r, s), xs.at[slot], xr.at[slot], to[d])

    def x_end(r):
        val = both(r, 0)
        for d in ("xp", "xm"):
            last = KX[d, r] - 1
            slot = XSLOT[d, r, last]
            recv(("s", d, r, last), xr.at[slot])
            val = val + xr[slot].astype(f32)
        return val

    zc("zp", 0, 0)
    zc("zm", 1, 0)
    zc("zp", 1, 0)
    zc("zm", 0, 0)
    for r, dx in CORDER:
        core_send(r, dx)

    ones = jnp.ones((16, T), bf16)
    second1 = dot_nt(ones, GH[...]) + dot_nt(ones, GL[...])
    second2 = dot_nn(ones, GH[...]) + dot_nn(ones, GL[...])
    lane_row = lax.broadcasted_iota(jnp.int32, (16, T), 0)

    def split_rows(M):
        s = jnp.concatenate([M[24:32, :], M[24:32, :]], axis=0)
        high = s.astype(bf16).astype(f32)
        low = s - high
        return jnp.where(lane_row == 0, high, jnp.where(lane_row == 1, low, 0.0)).astype(bf16)

    first1 = jnp.sum(dot_nt(split_rows(M2), G[...]), axis=0, keepdims=True) / B
    first2 = jnp.sum(dot_nn(split_rows(M1), G[...]), axis=0, keepdims=True) / B
    top = lane_row[0:8] == 0
    A1[0, :, 0:T] = jnp.where(top, jnp.broadcast_to(first1, (8, T)), second1[0:8])
    A1[0, :, T : T + 128] = loss_tile
    A2[0] = jnp.where(top, jnp.broadcast_to(first2, (8, T)), second2[0:8])

    def put(n):
        send(("a1", n), A1.at[n], R1.at[n], dp_steps[n])
        send(("a2", n), A2.at[n], R2.at[n], feat_steps[n])

    def take(n):
        recv(("a1", n), R1.at[n])
        recv(("a2", n), R2.at[n])
        A1[n + 1] = A1[n] + R1[n]
        A2[n + 1] = A2[n] + R2[n]

    put(0)
    xc("xp", 0, 0)
    xc("xm", 1, 0)
    zc("zp", 0, 1)
    zc("zm", 1, 1)
    take(0)
    put(1)
    xc("xp", 1, 0)
    xc("xm", 0, 0)
    zc("zp", 1, 1)
    zc("zm", 0, 1)
    take(1)
    put(2)
    xc("xp", 0, 1)
    xc("xm", 1, 1)
    zc("zp", 0, 2)
    zc("zm", 1, 2)
    take(2)
    put(3)
    ys[0] = x_end(1).astype(bf16)
    send(("s", "yl"), ys.at[0], yr.at[0], to_yl)
    zc("zp", 1, 2)
    zc("zm", 0, 2)
    take(3)

    def delta(U, V, M, A, D, i):
        stats = A[4]
        first = stats[0:1, 0:T] / B
        second = stats[1:2, 0:T] / B
        inv = M[16:17, :]

        def body(k, carry):
            off = pl.multiple_of(k * CH, 16)
            at_ = pl.ds(pl.multiple_of(i * R + k * CH, 16), CH)
            own = V[at_, :].astype(f32)
            D[at_, :] = (inv * (U[pl.ds(off, CH), :] / B - first - own * second)).astype(bf16)
            return carry

        lax.fori_loop(0, R // CH, body, 0)

    val = x_end(0)
    recv(("s", "yl"), yr.at[0])
    U1[...] = val + yr[0].astype(f32)
    delta(U1, V1, M1, A1, D1, dp)
    start_a("d", D1, at(D1, dp))
    zc("zp", 0, 3)
    zc("zm", 1, 3)

    AL[0] = A1[4, :, T : T + 128]

    def put_l(n):
        send(("al", n), AL.at[n], RL.at[n], feat_steps[n])

    def take_l(n):
        recv(("al", n), RL.at[n])
        AL[n + 1] = AL[n] + RL[n]

    put_l(0)
    ys[1] = z_end(1).astype(bf16)
    send(("s", "yh"), ys.at[1], yr.at[1], to_yh)
    ev_yl("d", D1)
    ev_x("d", D1, "xp", 0, 1)
    ev_x("d", D1, "xm", 0, 1)
    take_l(0)
    put_l(1)
    val = z_end(0)
    recv(("s", "yh"), yr.at[1])
    U2[...] = val + yr[1].astype(f32)
    delta(U2, V2, M2, A2, D2, ft)
    start_b("d", D2, at(D2, ft))

    ev_x("d", D1, "xp", 1, 1)
    ev_x("d", D1, "xm", 1, 1)
    ev_x("d", D1, "xp", 0, 2)
    ev_x("d", D1, "xm", 1, 2)
    take_l(1)
    put_l(2)
    ev_z("d", D2, "zp", 0, 1)
    ev_z("d", D2, "zm", 0, 1)
    take_l(2)
    put_l(3)
    ev_yh("d", D2)
    ev_z("d", D2, "zp", 0, 2)
    ev_z("d", D2, "zm", 0, 2)
    take_l(3)
    loss_ref[0] = jnp.sum(AL[4]) / F
    for r, dx in CORDER:
        ev_c("d", D1, r, dx)
    local[2].wait()
    local[3].wait()

    def weights(w_ref, X, D):
        w_ref[...] = dot_tn(X[0:KC, :], D[0:KC, :])

        def body(k, carry):
            at_ = pl.ds(pl.multiple_of(k * KC, 16), KC)
            w_ref[...] += dot_tn(X[at_, :], D[at_, :])
            return carry

        lax.fori_loop(1, B // KC, body, 0)

    ev_z("d", D2, "zp", 1, 1)
    ev_z("d", D2, "zm", 1, 1)
    ev_z("d", D2, "zp", 0, 3)
    ev_z("d", D2, "zm", 0, 3)
    weights(w1_ref, X1, D1)
    ev_z("d", D2, "zp", 1, 2)
    ev_z("d", D2, "zm", 1, 2)
    ev_z("d", D2, "zp", 0, 4)
    ev_z("d", D2, "zp", 1, 3)
    ev_z("d", D2, "zm", 1, 3)
    ev_z("d", D2, "zm", 1, 4)
    weights(w2_ref, X2, D2)
    drain()
    assert len(names) <= NSEM


def per_device(view_one, view_two, inputs_one, inputs_two, loss_scale):
    R, T = view_one.shape
    B = inputs_one.shape[0]
    block = (R, T)
    anywhere = pl.BlockSpec(memory_space=pl.ANY)
    vmem = pl.BlockSpec(memory_space=pltpu.VMEM)
    smem = pl.BlockSpec(memory_space=pltpu.SMEM)
    V = pltpu.VMEM
    scratch = [
        V((B, T), bf16), V((B, T), bf16), V((B, T), bf16), V((B, T), bf16),
        V((B, T), bf16), V((B, T), bf16),
        V((len(ZSLOT),) + block, bf16), V((len(ZSLOT),) + block, bf16),
        V((len(CSLOT),) + block, bf16), V((len(CSLOT),) + block, bf16),
        V((len(XSLOT),) + block, bf16), V((len(XSLOT),) + block, bf16),
        V((2,) + block, bf16), V((2,) + block, bf16),
        V(block, f32), V(block, f32),
        V((T, T), f32), V((T, T), bf16), V((T, T), bf16), V((T, T), bf16),
        V((32, T), f32), V((32, T), f32),
        V((5, 8, T + 128), f32), V((4, 8, T + 128), f32),
        V((5, 8, T), f32), V((4, 8, T), f32),
        V((5, 8, 128), f32), V((4, 8, 128), f32),
        pltpu.SemaphoreType.DMA((NSEM,)),
        pltpu.SemaphoreType.DMA((NSEM,)),
        pltpu.SemaphoreType.DMA((4,)),
    ]
    return pl.pallas_call(
        kernel,
        out_shape=(
            jax.ShapeDtypeStruct((1,), f32),
            jax.ShapeDtypeStruct((T, T), f32),
            jax.ShapeDtypeStruct((T, T), f32),
        ),
        in_specs=[anywhere] * 4 + [smem],
        out_specs=(smem, vmem, vmem),
        scratch_shapes=scratch,
        compiler_params=pltpu.CompilerParams(
            collective_id=0, has_side_effects=True, vmem_limit_bytes=58 * 1024 * 1024
        ),
        cost_estimate=pl.CostEstimate(
            flops=10 * B * T * T, bytes_accessed=4 * B * T + 8 * T * T, transcendentals=0
        ),
    )(view_one, view_two, inputs_one, inputs_two, loss_scale)


def solution(mesh):
    placed = (P("dp", "feat"), P("feat", "dp"), P(None, "dp"), P(None, "feat"), P())
    return jax.shard_map(
        per_device,
        mesh=mesh,
        in_specs=placed,
        out_specs=(P(), P("dp", "feat"), P("feat", "dp")),
        check_vma=False,
    )
```

```python
import jax
import jax.numpy as jnp
from jax import lax
from jax.experimental import pallas as pl
from jax.experimental.pallas import tpu as pltpu
from jax.sharding import PartitionSpec as P

F = 8192
off_weight = 0.0051
epsilon = 1e-05
MESH = pl.DeviceIdType.MESH
f32 = jnp.float32
bf16 = jnp.bfloat16

NX = 4
NZ = 8
SIGN = {"xp": 1, "xm": -1}
KX = {("xp", 0): 2, ("xm", 0): 1, ("xp", 1): 1, ("xm", 1): 2}
PIECES = ((0, 128), (128, 112))
ZSLOT = {
    key: n
    for n, key in enumerate(
        [(1, 4), (1, 3), (1, -3), (1, -2), (0, 4), (0, 3), (0, 2), (0, 1), (0, -3), (0, -2), (0, -1)]
        + [("y", 2), ("y", -1), ("y", 1), ("y", 0)]
    )
}
XSLOT = {}
for key, hops in KX.items():
    for hop in range(hops):
        XSLOT[key + (hop,)] = len(XSLOT)
CORDER = [(0, 2), (1, 2), (1, 1), (0, 3), (0, 1), (1, 3), (1, 0), (0, 0)]
CSLOT = {key: n for n, key in enumerate(CORDER)}
NSEM = 200


def dot_tn(left, right):
    return lax.dot_general(left, right, (((0,), (0,)), ((), ())), preferred_element_type=f32)


def dot_nt(left, right):
    return lax.dot_general(left, right, (((1,), (1,)), ((), ())), preferred_element_type=f32)


def dot_nn(left, right):
    return lax.dot_general(left, right, (((1,), (0,)), ((), ())), preferred_element_type=f32)


def fold8(block):
    total = block[0:8]
    for k in range(8, block.shape[0], 8):
        total = total + block[k : k + 8]
    return total


def kernel(
    view1, view2, in1, in2, scale_ref,
    loss_ref, w1_ref, w2_ref,
    V1, V2, D1, D2, X1, X2,
    zs, zr, cs, cr, xs, xr, ys, yr, U1, U2,
    C, G, GH, GL, M1, M2, A1, R1, A2, R2, AL, RL,
    ssem, rsem, lsem,
):
    R = view1.shape[0]
    B = V1.shape[0]
    T = V1.shape[1]
    dp = lax.axis_index("dp")
    ft = lax.axis_index("feat")
    c = lax.rem(dp, 2)
    x = lax.rem(lax.div(dp, 2), NX)
    yl = lax.div(dp, 2 * NX)
    yh = lax.rem(ft, 2)
    z = lax.div(ft, 2)

    def dpi(r, dx, other=0):
        y_ = yl if r == 0 else 1 - yl
        c_ = 1 - c if other else c
        return (y_ * NX + lax.rem(x + (dx % NX), NX)) * 2 + c_

    turn = 1 - 2 * c

    def fti(r, dz):
        y_ = yh if r == 0 else 1 - yh
        return lax.rem(z + NZ + dz * turn, NZ) * 2 + y_

    def rows(i):
        return pl.ds(pl.multiple_of(i * R, 16), R)

    def at(buf, i, u=None):
        if u is None:
            return buf.at[rows(i)]
        return buf.at[pl.ds(pl.multiple_of(i * R + PIECES[u][0], 16), PIECES[u][1])]

    def part(buf, slot, u):
        return buf.at[slot, pl.ds(*PIECES[u])]

    to_core = {"dp": dpi(0, 0, 1), "feat": ft}
    to_yl = {"dp": dpi(1, 0), "feat": ft}
    to_yh = {"dp": dp, "feat": fti(1, 0)}
    to = {
        "xp": {"dp": dpi(0, 1), "feat": ft},
        "xm": {"dp": dpi(0, -1), "feat": ft},
        "p": {"dp": dp, "feat": fti(0, 1)},
        "m": {"dp": dp, "feat": fti(0, -1)},
    }
    xa = x + 1 - 2 * lax.rem(x, 2)
    xb = NX - 1 - x
    za = z + 1 - 2 * lax.rem(z, 2)
    zb = z + 2 - 4 * lax.rem(lax.div(z, 2), 2)
    dp_steps = [
        to_core,
        to_yl,
        {"dp": (yl * NX + xa) * 2 + c, "feat": ft},
        {"dp": (yl * NX + xb) * 2 + c, "feat": ft},
    ]
    to_zb = {"dp": dp, "feat": zb * 2 + yh}
    to_zc = {"dp": dp, "feat": fti(0, 4)}
    feat_steps = [to_yh, {"dp": dp, "feat": za * 2 + yh}, to_zb, to_zc]

    peers = [to_core, to_yl, to_yh, to["xp"], to["xm"], to["p"], to["m"], to_zb, to_zc]
    barrier = pltpu.get_barrier_semaphore()
    for peer in peers:
        pl.semaphore_signal(barrier, inc=1, device_id=peer, device_id_type=MESH)
    local = [
        pltpu.make_async_copy(view1, at(V1, dp), lsem.at[0]),
        pltpu.make_async_copy(view2, at(V2, ft), lsem.at[1]),
        pltpu.make_async_copy(in1, X1, lsem.at[2]),
        pltpu.make_async_copy(in2, X2, lsem.at[3]),
    ]
    for copy in local:
        copy.start()
    pl.semaphore_wait(barrier, len(peers))

    names = {}
    flying = {}

    def index(name):
        return names.setdefault(name, len(names))

    def send(name, src, dst, dev):
        k = index(name)
        copy = pltpu.make_async_remote_copy(
            src_ref=src, dst_ref=dst, send_sem=ssem.at[k], recv_sem=rsem.at[k],
            device_id=dev, device_id_type=MESH,
        )
        copy.start()
        flying[name] = copy

    def recv(name, dst):
        k = index(name)
        pltpu.make_async_remote_copy(
            src_ref=dst, dst_ref=dst, send_sem=ssem.at[k], recv_sem=rsem.at[k],
            device_id=to_core, device_id_type=MESH,
        ).wait_recv()

    def drain(keep=lambda name: True):
        for name in [n for n in flying if keep(n)]:
            flying.pop(name).wait_send()

    def start_a(tag, A, src):
        own = at(A, dp)
        send((tag, "yl"), src, own, to_yl)
        send((tag, "xp", 0, 1), src, own, to["xp"])
        send((tag, "xm", 0, 1), src, own, to["xm"])
        send((tag, "c", 0, 0), src, own, to_core)

    def start_b(tag, Bb, src):
        own = at(Bb, ft)
        for u in range(len(PIECES)):
            piece = src.at[pl.ds(*PIECES[u])]
            for d in ("p", "m"):
                send((tag, d, 0, 1, u), piece, at(Bb, ft, u), to[d])
        send((tag, "y", 0), src, own, to_yh)

    def ev_yl(tag, A):
        i = dpi(1, 0)
        recv((tag, "yl"), at(A, i))
        send((tag, "xp", 1, 1), at(A, i), at(A, i), to["xp"])
        send((tag, "xm", 1, 1), at(A, i), at(A, i), to["xm"])
        send((tag, "c", 1, 0), at(A, i), at(A, i), to_core)
        return i

    def ev_y0(tag, Bb):
        recv((tag, "y", 0), at(Bb, fti(1, 0)))

    def ev_x(tag, A, d, r, h):
        dx = (-SIGN[d] * h) % NX
        i = dpi(r, dx)
        recv((tag, d, r, h), at(A, i))
        if h < KX[d, r]:
            send((tag, d, r, h + 1), at(A, i), at(A, i), to[d])
        send((tag, "c", r, dx), at(A, i), at(A, i), to_core)
        return i

    def ev_z(tag, Bb, d, r, h):
        sign = 1 if d == "p" else -1
        i = fti(r, -sign * h)
        for u in range(len(PIECES)):
            piece = at(Bb, i, u)
            recv((tag, d, r, h, u), piece)
            if h < (4 if d == "p" else 3):
                send((tag, d, r, h + 1, u), piece, piece, to[d])
            if r == 0 and (d, h) in (("m", 1), ("p", 2)):
                send((tag, "y", d, h, u), piece, piece, to_yh)
        if r == 0 and (d, h) == ("p", 2):
            early = at(Bb, fti(0, -1))
            send((tag, "y", "p", 1), early, early, to_yh)
        return i

    def ev_y(tag, Bb, d, h):
        sign = 1 if d == "p" else -1
        i = fti(1, -sign * h)
        if (d, h) == ("p", 1):
            recv((tag, "y", d, h), at(Bb, i))
            return i
        for u in range(len(PIECES)):
            piece = at(Bb, i, u)
            recv((tag, "y", d, h, u), piece)
            send((tag, d, 1, h + 1, u), piece, piece, to[d])
        return i

    def ev_c(tag, A, r, dx):
        i = dpi(r, dx, 1)
        recv((tag, "c", r, dx), at(A, i))
        return i

    CH = 48

    def moments(V, M, i):
        base = i * R

        def body(k, carry):
            s, q = carry
            v = V[pl.ds(pl.multiple_of(base + k * CH, 16), CH), :].astype(f32)
            return s + fold8(v), q + fold8(v * v)

        s, q = lax.fori_loop(0, R // CH, body, (M[0:8, :], M[8:16, :]))
        M[0:8, :] = s
        M[8:16, :] = q

    def normalize(V, M):
        average = jnp.sum(M[0:8, :], axis=0, keepdims=True) / B
        spread = jnp.sum(M[8:16, :], axis=0, keepdims=True) / B - average * average
        inv = lax.rsqrt(spread + epsilon)
        M[16:24, :] = jnp.broadcast_to(inv, (8, T))

        def body(k, total):
            at_ = pl.ds(pl.multiple_of(k * CH, 16), CH)
            n = ((V[at_, :].astype(f32) - average) * inv).astype(bf16)
            V[at_, :] = n
            return total + fold8(n.astype(f32))

        total = lax.fori_loop(0, B // CH, body, jnp.zeros((8, T), f32))
        M[24:32, :] = jnp.broadcast_to(jnp.sum(total, axis=0, keepdims=True), (8, T))

    M1[...] = jnp.zeros_like(M1)
    M2[...] = jnp.zeros_like(M2)
    start_b("g", V2, view2)
    start_a("g", V1, view1)
    local[0].wait()
    local[1].wait()
    moments(V1, M1, dp)
    moments(V2, M2, ft)

    def gz(d, r, h):
        moments(V2, M2, ev_z("g", V2, d, r, h))

    def gx(d, r, h):
        moments(V1, M1, ev_x("g", V1, d, r, h))

    def gc(r, dx):
        moments(V1, M1, ev_c("g", V1, r, dx))

    gz("p", 0, 1)
    gz("m", 0, 1)
    moments(V1, M1, ev_yl("g", V1))
    gx("xp", 0, 1)
    gx("xm", 0, 1)
    ev_y0("g", V2)
    moments(V2, M2, fti(1, 0))
    gz("p", 0, 2)
    gz("m", 0, 2)
    gx("xp", 1, 1)
    gx("xm", 1, 1)
    moments(V2, M2, ev_y("g", V2, "m", 1))
    gx("xp", 0, 2)
    gx("xm", 1, 2)
    gz("p", 0, 3)
    gz("m", 0, 3)
    for r, dx in CORDER:
        gc(r, dx)
    gz("m", 1, 2)
    moments(V2, M2, ev_y("g", V2, "p", 2))
    moments(V2, M2, ev_y("g", V2, "p", 1))
    gz("p", 0, 4)
    gz("p", 1, 3)
    gz("m", 1, 3)
    drain(lambda n: n[1] in ("c", "xp", "xm", "yl"))
    normalize(V1, M1)
    gz("p", 1, 4)
    drain()
    normalize(V2, M2)

    KC = 768
    C[...] = dot_tn(V1[0:KC, :], V2[0:KC, :])

    def corr(k, carry):
        at_ = pl.ds(pl.multiple_of(k * KC, 16), KC)
        C[...] += dot_tn(V1[at_, :], V2[at_, :])
        return carry

    lax.fori_loop(1, B // KC, corr, 0)

    CG = 32
    scale = scale_ref[0]
    row0 = ft * T
    col0 = dp * T

    def grad(k, loss):
        at_ = pl.ds(pl.multiple_of(k * CG, CG), CG)
        corr_ = C[at_, :] / B
        row_ids = row0 + k * CG + lax.broadcasted_iota(jnp.int32, (CG, T), 0)
        col_ids = col0 + lax.broadcasted_iota(jnp.int32, (CG, T), 1)
        on = row_ids == col_ids
        miss = 1.0 - corr_
        loss = loss + fold8(jnp.where(on, miss * miss, off_weight * corr_ * corr_))
        g = (jnp.where(on, -2.0 * miss, 2.0 * off_weight * corr_) * scale).astype(bf16)
        G[at_, :] = g
        prod = g.astype(f32) * corr_
        high = prod.astype(bf16)
        GH[at_, :] = high
        GL[at_, :] = (prod - high.astype(f32)).astype(bf16)
        return loss

    loss = lax.fori_loop(0, T // CG, grad, jnp.zeros((8, T), f32))
    loss_tile = loss[:, 0:128]
    for k in range(128, T, 128):
        loss_tile = loss_tile + loss[:, k : k + 128]

    def p2(i, u):
        return dot_nn(V1[pl.ds(pl.multiple_of(i * R + PIECES[u][0], 16), PIECES[u][1]), :], G[...])

    def p1(i):
        return dot_nt(V2[rows(i), :], G[...])

    def arrived(key, u):
        slot = ZSLOT[key]
        recv(("s", key, u), part(zr, slot, u))
        return part(zr, slot, u)[...].astype(f32)

    def zc(r, k, over_y=False, take=()):
        key = ("y", k) if over_y else (r, k)
        dev = to_yh if over_y else to["m"] if k > 0 else to["p"]
        for u in range(len(PIECES)):
            val = p2(fti(r, -k), u)
            for source in take:
                val = val + arrived(source, u)
            part(zs, ZSLOT[key], u)[...] = val.astype(bf16)
            send(("s", key, u), part(zs, ZSLOT[key], u), part(zr, ZSLOT[key], u), dev)

    def z_end():
        for u in range(len(PIECES)):
            val = p2(fti(0, 0), u)
            for source in ((0, 1), (0, -1), ("y", 0)):
                val = val + arrived(source, u)
            U2[pl.ds(*PIECES[u]), :] = val

    def core_send(r, dx):
        slot = CSLOT[r, dx]
        cs[slot] = p1(dpi(r, dx, 1)).astype(bf16)
        send(("s", "c", r, dx), cs.at[slot], cr.at[slot], to_core)

    def both(r, dx):
        dx = dx % NX
        val = p1(dpi(r, dx))
        slot = CSLOT[r, dx]
        recv(("s", "c", r, dx), cr.at[slot])
        return val + cr[slot].astype(f32)

    def xc(d, r, s):
        val = both(r, SIGN[d] * (KX[d, r] - s))
        if s:
            prev = XSLOT[d, r, s - 1]
            recv(("s", d, r, s - 1), xr.at[prev])
            val = val + xr[prev].astype(f32)
        slot = XSLOT[d, r, s]
        xs[slot] = val.astype(bf16)
        send(("s", d, r, s), xs.at[slot], xr.at[slot], to[d])

    def x_end(r):
        val = both(r, 0)
        for d in ("xp", "xm"):
            last = KX[d, r] - 1
            slot = XSLOT[d, r, last]
            recv(("s", d, r, last), xr.at[slot])
            val = val + xr[slot].astype(f32)
        return val

    zc(1, 4)
    zc(1, -3)
    zc(0, 4)
    zc(0, -3)
    for r, dx in CORDER:
        core_send(r, dx)

    ones = jnp.ones((16, T), bf16)
    second1 = dot_nt(ones, GH[...]) + dot_nt(ones, GL[...])
    second2 = dot_nn(ones, GH[...]) + dot_nn(ones, GL[...])
    lane_row = lax.broadcasted_iota(jnp.int32, (16, T), 0)

    def split_rows(M):
        s = jnp.concatenate([M[24:32, :], M[24:32, :]], axis=0)
        high = s.astype(bf16).astype(f32)
        low = s - high
        return jnp.where(lane_row == 0, high, jnp.where(lane_row == 1, low, 0.0)).astype(bf16)

    first1 = jnp.sum(dot_nt(split_rows(M2), G[...]), axis=0, keepdims=True) / B
    first2 = jnp.sum(dot_nn(split_rows(M1), G[...]), axis=0, keepdims=True) / B
    top = lane_row[0:8] == 0
    A1[0, :, 0:T] = jnp.where(top, jnp.broadcast_to(first1, (8, T)), second1[0:8])
    A1[0, :, T : T + 128] = loss_tile
    A2[0] = jnp.where(top, jnp.broadcast_to(first2, (8, T)), second2[0:8])

    def put(n):
        send(("a1", n), A1.at[n], R1.at[n], dp_steps[n])
        send(("a2", n), A2.at[n], R2.at[n], feat_steps[n])

    def take(n):
        recv(("a1", n), R1.at[n])
        recv(("a2", n), R2.at[n])
        A1[n + 1] = A1[n] + R1[n]
        A2[n + 1] = A2[n] + R2[n]

    put(0)
    xc("xp", 0, 0)
    xc("xm", 1, 0)
    zc(1, 1, True)
    zc(1, 3, take=[(1, 4)])
    zc(1, -2, take=[(1, -3)])
    take(0)
    put(1)
    xc("xp", 1, 0)
    xc("xm", 0, 0)
    zc(0, 3, take=[(0, 4)])
    zc(0, -2, take=[(0, -3)])
    take(1)
    put(2)
    zc(1, 2, True, take=[(1, 3)])
    zc(1, -1, True, take=[(1, -2)])
    xc("xp", 0, 1)
    xc("xm", 1, 1)
    take(2)
    put(3)
    zc(1, 0, True)
    ys[0] = x_end(1).astype(bf16)
    send(("s", "yl"), ys.at[0], yr.at[0], to_yl)
    zc(0, 2, take=[(0, 3), ("y", 2)])
    zc(0, -1, take=[(0, -2), ("y", -1)])
    take(3)

    def delta(U, V, M, A, D, i):
        stats = A[4]
        first = stats[0:1, 0:T] / B
        second = stats[1:2, 0:T] / B
        inv = M[16:17, :]

        def body(k, carry):
            off = pl.multiple_of(k * CH, 16)
            at_ = pl.ds(pl.multiple_of(i * R + k * CH, 16), CH)
            own = V[at_, :].astype(f32)
            D[at_, :] = (inv * (U[pl.ds(off, CH), :] / B - first - own * second)).astype(bf16)
            return carry

        lax.fori_loop(0, R // CH, body, 0)

    val = x_end(0)
    recv(("s", "yl"), yr.at[0])
    U1[...] = val + yr[0].astype(f32)
    delta(U1, V1, M1, A1, D1, dp)
    start_a("d", D1, at(D1, dp))
    zc(0, 1, take=[(0, 2), ("y", 1)])

    AL[0] = A1[4, :, T : T + 128]

    def put_l(n):
        send(("al", n), AL.at[n], RL.at[n], feat_steps[n])

    def take_l(n):
        recv(("al", n), RL.at[n])
        AL[n + 1] = AL[n] + RL[n]

    put_l(0)
    ev_yl("d", D1)
    ev_x("d", D1, "xp", 0, 1)
    ev_x("d", D1, "xm", 0, 1)
    take_l(0)
    put_l(1)
    z_end()
    delta(U2, V2, M2, A2, D2, ft)
    start_b("d", D2, at(D2, ft))

    ev_x("d", D1, "xp", 1, 1)
    ev_x("d", D1, "xm", 1, 1)
    ev_x("d", D1, "xp", 0, 2)
    ev_x("d", D1, "xm", 1, 2)
    take_l(1)
    put_l(2)
    local[2].wait()
    local[3].wait()

    def weight(w_ref, X, D, i, first=False):
        term = dot_tn(X[rows(i), :], D[rows(i), :])
        if first:
            w_ref[...] = term
        else:
            w_ref[...] += term

    def dz(d, r, h):
        weight(w2_ref, X2, D2, ev_z("d", D2, d, r, h))

    def dy(d, h):
        weight(w2_ref, X2, D2, ev_y("d", D2, d, h))

    weight(w2_ref, X2, D2, ft, True)
    dz("p", 0, 1)
    dz("m", 0, 1)
    take_l(2)
    put_l(3)
    ev_y0("d", D2)
    weight(w2_ref, X2, D2, fti(1, 0))
    for r, dx in CORDER:
        ev_c("d", D1, r, dx)
    dz("p", 0, 2)
    dz("m", 0, 2)
    take_l(3)
    loss_ref[0] = jnp.sum(AL[4]) / F
    dy("m", 1)
    dz("p", 0, 3)
    dz("m", 0, 3)
    w1_ref[...] = dot_tn(X1[0:KC, :], D1[0:KC, :])

    def body(k, carry):
        at_ = pl.ds(pl.multiple_of(k * KC, 16), KC)
        w1_ref[...] += dot_tn(X1[at_, :], D1[at_, :])
        return carry

    lax.fori_loop(1, B // KC, body, 0)
    dz("m", 1, 2)
    dy("p", 2)
    dy("p", 1)
    dz("p", 0, 4)
    dz("p", 1, 3)
    dz("m", 1, 3)
    dz("p", 1, 4)
    drain()
    assert len(names) <= NSEM


def per_device(view_one, view_two, inputs_one, inputs_two, loss_scale):
    R, T = view_one.shape
    B = inputs_one.shape[0]
    block = (R, T)
    anywhere = pl.BlockSpec(memory_space=pl.ANY)
    vmem = pl.BlockSpec(memory_space=pltpu.VMEM)
    smem = pl.BlockSpec(memory_space=pltpu.SMEM)
    V = pltpu.VMEM
    scratch = [
        V((B, T), bf16), V((B, T), bf16), V((B, T), bf16), V((B, T), bf16),
        V((B, T), bf16), V((B, T), bf16),
        V((len(ZSLOT),) + block, bf16), V((len(ZSLOT),) + block, bf16),
        V((len(CSLOT),) + block, bf16), V((len(CSLOT),) + block, bf16),
        V((len(XSLOT),) + block, bf16), V((len(XSLOT),) + block, bf16),
        V((2,) + block, bf16), V((2,) + block, bf16),
        V(block, f32), V(block, f32),
        V((T, T), f32), V((T, T), bf16), V((T, T), bf16), V((T, T), bf16),
        V((32, T), f32), V((32, T), f32),
        V((5, 8, T + 128), f32), V((4, 8, T + 128), f32),
        V((5, 8, T), f32), V((4, 8, T), f32),
        V((5, 8, 128), f32), V((4, 8, 128), f32),
        pltpu.SemaphoreType.DMA((NSEM,)),
        pltpu.SemaphoreType.DMA((NSEM,)),
        pltpu.SemaphoreType.DMA((4,)),
    ]
    return pl.pallas_call(
        kernel,
        out_shape=(
            jax.ShapeDtypeStruct((1,), f32),
            V((T, T), f32),
            V((T, T), f32),
        ),
        in_specs=[anywhere] * 4 + [smem],
        out_specs=(smem, vmem, vmem),
        scratch_shapes=scratch,
        compiler_params=pltpu.CompilerParams(
            collective_id=0, has_side_effects=True, vmem_limit_bytes=58 * 1024 * 1024
        ),
        cost_estimate=pl.CostEstimate(
            flops=10 * B * T * T, bytes_accessed=4 * B * T + 8 * T * T, transcendentals=0
        ),
    )(view_one, view_two, inputs_one, inputs_two, loss_scale)


def solution(mesh):
    placed = (P("dp", "feat"), P("feat", "dp"), P(None, "dp"), P(None, "feat"), P())
    return jax.shard_map(
        per_device,
        mesh=mesh,
        in_specs=placed,
        out_specs=(P(), P("dp", "feat"), P("feat", "dp")),
        check_vma=False,
    )
```

```python
import jax
import jax.numpy as jnp
from jax import lax
from jax.experimental import pallas as pl
from jax.experimental.pallas import tpu as pltpu
from jax.sharding import PartitionSpec as P

F = 8192
off_weight = 0.0051
epsilon = 1e-05
MESH = pl.DeviceIdType.MESH
f32 = jnp.float32
bf16 = jnp.bfloat16

NX = 4
NZ = 8
SIGN = {"xp": 1, "xm": -1}
KX = {("xp", 0): 2, ("xm", 0): 1, ("xp", 1): 1, ("xm", 1): 2}
PIECES = ((0, 128), (128, 112))
NP = len(PIECES)
ZSLOT = {
    key: n
    for n, key in enumerate(
        [(1, 4), (1, 3), (1, -3), (1, -2), (0, 4), (0, 3), (0, 2), (0, 1), (0, -3), (0, -2), (0, -1)]
        + [("y", 2), ("y", -1), ("y", 1), ("y", 0)]
    )
}
XSLOT = {}
for key, hops in KX.items():
    for hop in range(hops):
        XSLOT[key + (hop,)] = len(XSLOT)
CORDER = [(0, 2), (1, 2), (1, 1), (0, 3), (0, 1), (1, 3), (1, 0), (0, 0)]
CSLOT = {key: n for n, key in enumerate(CORDER)}
NSEM = 240

def both_z(r, hp, hm):
    return [("z", d, r, h, u) for u in range(NP) for d, h in (("p", hp), ("m", hm)) if h]


def one_z(d, r, h):
    return [("z", d, r, h, u) for u in range(NP)]


def over_y(d, h):
    return [("y", d, h, u) for u in range(NP)]


ORDER = (
    both_z(0, 1, 1)
    + [("yl",), ("x", "xp", 0, 1), ("x", "xm", 0, 1)]
    + both_z(0, 2, 2)
    + [("x", "xp", 1, 1), ("x", "xm", 1, 1)]
    + over_y("m", 1)
    + [("ls", 0)]
    + both_z(0, 3, 3)
    + [("x", "xp", 0, 2), ("x", "xm", 1, 2)]
    + over_y("p", 2)
    + [("ls", 1)]
    + one_z("m", 1, 2)
    + [("c", r, dx) for r, dx in CORDER]
    + one_z("p", 0, 4)
    + one_z("p", 1, 3)
    + one_z("m", 1, 3)
    + [("lr", 0), ("lr", 1)]
    + one_z("p", 1, 4)
)
NORM = len(ORDER) - 2 - 4 * NP


def dot_tn(left, right):
    return lax.dot_general(left, right, (((0,), (0,)), ((), ())), preferred_element_type=f32)


def dot_nt(left, right):
    return lax.dot_general(left, right, (((1,), (1,)), ((), ())), preferred_element_type=f32)


def dot_nn(left, right):
    return lax.dot_general(left, right, (((1,), (0,)), ((), ())), preferred_element_type=f32)


def fold8(block):
    total = block[0:8]
    for k in range(8, block.shape[0], 8):
        total = total + block[k : k + 8]
    return total


def kernel(
    view1, view2, in1, in2, scale_ref,
    loss_ref, w1_ref, w2_ref,
    V1, V2, D1, D2, X1, X2,
    zs, zr, cs, cr, xs, xr, ys, yr, U1, U2,
    C, G, GH, GL, M1, M2, A1, R1, A2, R2, AL, RL,
    ssem, rsem, lsem,
):
    R = view1.shape[0]
    B = V1.shape[0]
    T = V1.shape[1]
    dp = lax.axis_index("dp")
    ft = lax.axis_index("feat")
    c = lax.rem(dp, 2)
    x = lax.rem(lax.div(dp, 2), NX)
    yl = lax.div(dp, 2 * NX)
    yh = lax.rem(ft, 2)
    z = lax.div(ft, 2)

    def dpi(r, dx, other=0):
        y_ = yl if r == 0 else 1 - yl
        c_ = 1 - c if other else c
        return (y_ * NX + lax.rem(x + (dx % NX), NX)) * 2 + c_

    turn = 1 - 2 * c

    def fti(r, dz):
        y_ = yh if r == 0 else 1 - yh
        return lax.rem(z + NZ + dz * turn, NZ) * 2 + y_

    def rows(i):
        return pl.ds(pl.multiple_of(i * R, 16), R)

    def at(buf, i, u=None):
        if u is None:
            return buf.at[rows(i)]
        return buf.at[pl.ds(pl.multiple_of(i * R + PIECES[u][0], 16), PIECES[u][1])]

    def part(buf, slot, u):
        return buf.at[slot, pl.ds(*PIECES[u])]

    to_core = {"dp": dpi(0, 0, 1), "feat": ft}
    to_yl = {"dp": dpi(1, 0), "feat": ft}
    to_yh = {"dp": dp, "feat": fti(1, 0)}
    to = {
        "xp": {"dp": dpi(0, 1), "feat": ft},
        "xm": {"dp": dpi(0, -1), "feat": ft},
        "p": {"dp": dp, "feat": fti(0, 1)},
        "m": {"dp": dp, "feat": fti(0, -1)},
    }
    xa = x + 1 - 2 * lax.rem(x, 2)
    xb = NX - 1 - x
    za = z + 1 - 2 * lax.rem(z, 2)
    zb = z + 2 - 4 * lax.rem(lax.div(z, 2), 2)
    dp_steps = [
        to_core,
        to_yl,
        {"dp": (yl * NX + xa) * 2 + c, "feat": ft},
        {"dp": (yl * NX + xb) * 2 + c, "feat": ft},
    ]
    to_zb = {"dp": dp, "feat": zb * 2 + yh}
    to_zc = {"dp": dp, "feat": fti(0, 4)}
    feat_steps = [to_yh, {"dp": dp, "feat": za * 2 + yh}, to_zb, to_zc]

    peers = [to_core, to_yl, to_yh, to["xp"], to["xm"], to["p"], to["m"], to_zb, to_zc]
    barrier = pltpu.get_barrier_semaphore()
    for peer in peers:
        pl.semaphore_signal(barrier, inc=1, device_id=peer, device_id_type=MESH)
    local = [
        pltpu.make_async_copy(view1, at(V1, dp), lsem.at[0]),
        pltpu.make_async_copy(view2, at(V2, ft), lsem.at[1]),
        pltpu.make_async_copy(in1, X1, lsem.at[2]),
        pltpu.make_async_copy(in2, X2, lsem.at[3]),
    ]
    for copy in local:
        copy.start()
    pl.semaphore_wait(barrier, len(peers))

    names = {}
    flying = {}

    def index(name):
        return names.setdefault(name, len(names))

    def send(name, src, dst, dev):
        k = index(name)
        copy = pltpu.make_async_remote_copy(
            src_ref=src, dst_ref=dst, send_sem=ssem.at[k], recv_sem=rsem.at[k],
            device_id=dev, device_id_type=MESH,
        )
        copy.start()
        flying[name] = copy

    def recv(name, dst):
        k = index(name)
        pltpu.make_async_remote_copy(
            src_ref=dst, dst_ref=dst, send_sem=ssem.at[k], recv_sem=rsem.at[k],
            device_id=to_core, device_id_type=MESH,
        ).wait_recv()

    def drain(keep=lambda name: True):
        for name in [n for n in flying if keep(n)]:
            flying.pop(name).wait_send()

    def start_a(tag, A, src):
        own = at(A, dp)
        send((tag, "yl"), src, own, to_yl)
        send((tag, "xp", 0, 1), src, own, to["xp"])
        send((tag, "xm", 0, 1), src, own, to["xm"])
        send((tag, "c", 0, 0), src, own, to_core)

    def start_b(tag, Bb, src):
        for u in range(len(PIECES)):
            for d in ("p", "m"):
                send((tag, d, 0, 1, u), src.at[pl.ds(*PIECES[u])], at(Bb, ft, u), to[d])

    def ev_yl(tag, A):
        i = dpi(1, 0)
        recv((tag, "yl"), at(A, i))
        send((tag, "xp", 1, 1), at(A, i), at(A, i), to["xp"])
        send((tag, "xm", 1, 1), at(A, i), at(A, i), to["xm"])
        send((tag, "c", 1, 0), at(A, i), at(A, i), to_core)
        return i

    def ev_z(tag, Bb, d, r, h, u):
        i = fti(r, -h if d == "p" else h)
        piece = at(Bb, i, u)
        recv((tag, d, r, h, u), piece)
        if r == 0 and (d, h) in (("m", 1), ("p", 2)):
            send((tag, "y", d, h, u), piece, piece, to_yh)
        if h < (4 if d == "p" else 3):
            send((tag, d, r, h + 1, u), piece, piece, to[d])
        return i

    def ev_y(tag, Bb, d, h, u):
        i = fti(1, -h if d == "p" else h)
        piece = at(Bb, i, u)
        recv((tag, "y", d, h, u), piece)
        send((tag, d, 1, h + 1, u), piece, piece, to[d])
        return i

    def ev_x(tag, A, d, r, h):
        dx = (-SIGN[d] * h) % NX
        i = dpi(r, dx)
        recv((tag, d, r, h), at(A, i))
        if h < KX[d, r]:
            send((tag, d, r, h + 1), at(A, i), at(A, i), to[d])
        send((tag, "c", r, dx), at(A, i), at(A, i), to_core)
        return i

    def late_send(tag, Bb, n):
        block = at(Bb, fti(0, -n))
        send((tag, "y", n), block, block, to_yh)

    def late_recv(tag, Bb, n):
        i = fti(1, -n)
        recv((tag, "y", n), at(Bb, i))
        return i

    def gather(order, tag, A, Bb, hook_a, hook_b):
        last = len(PIECES) - 1
        for ev in order:
            kind, args = ev[0], ev[1:]
            if kind == "z":
                i = ev_z(tag, Bb, *args)
                if args[-1] == last:
                    hook_b(i)
            elif kind == "y":
                i = ev_y(tag, Bb, *args)
                if args[-1] == last:
                    hook_b(i)
            elif kind == "ls":
                late_send(tag, Bb, *args)
            elif kind == "lr":
                hook_b(late_recv(tag, Bb, *args))
            elif kind == "yl":
                hook_a(ev_yl(tag, A))
            elif kind == "x":
                hook_a(ev_x(tag, A, *args))
            elif kind == "c":
                hook_a(ev_c(tag, A, *args))
            else:
                kind()

    def ev_c(tag, A, r, dx):
        i = dpi(r, dx, 1)
        recv((tag, "c", r, dx), at(A, i))
        return i

    CH = 48

    def moments(V, M, i):
        base = i * R

        def body(k, carry):
            s, q = carry
            v = V[pl.ds(pl.multiple_of(base + k * CH, 16), CH), :].astype(f32)
            return s + fold8(v), q + fold8(v * v)

        s, q = lax.fori_loop(0, R // CH, body, (M[0:8, :], M[8:16, :]))
        M[0:8, :] = s
        M[8:16, :] = q

    def normalize(V, M):
        average = jnp.sum(M[0:8, :], axis=0, keepdims=True) / B
        spread = jnp.sum(M[8:16, :], axis=0, keepdims=True) / B - average * average
        inv = lax.rsqrt(spread + epsilon)
        M[16:24, :] = jnp.broadcast_to(inv, (8, T))

        def body(k, total):
            at_ = pl.ds(pl.multiple_of(k * CH, 16), CH)
            n = ((V[at_, :].astype(f32) - average) * inv).astype(bf16)
            V[at_, :] = n
            return total + fold8(n.astype(f32))

        total = lax.fori_loop(0, B // CH, body, jnp.zeros((8, T), f32))
        M[24:32, :] = jnp.broadcast_to(jnp.sum(total, axis=0, keepdims=True), (8, T))

    M1[...] = jnp.zeros_like(M1)
    M2[...] = jnp.zeros_like(M2)
    start_b("g", V2, view2)
    start_a("g", V1, view1)
    local[0].wait()
    local[1].wait()
    moments(V1, M1, dp)
    moments(V2, M2, ft)

    def early_normalize():
        drain(lambda n: n[1] in ("c", "xp", "xm", "yl"))
        normalize(V1, M1)

    order = ORDER[:NORM] + [(early_normalize,)] + ORDER[NORM:]
    gather(order, "g", V1, V2, lambda i: moments(V1, M1, i), lambda i: moments(V2, M2, i))
    drain()
    normalize(V2, M2)

    KC = 768
    C[...] = dot_tn(V1[0:KC, :], V2[0:KC, :])

    def corr(k, carry):
        at_ = pl.ds(pl.multiple_of(k * KC, 16), KC)
        C[...] += dot_tn(V1[at_, :], V2[at_, :])
        return carry

    lax.fori_loop(1, B // KC, corr, 0)

    CG = 32
    scale = scale_ref[0]
    row0 = ft * T
    col0 = dp * T

    def grad(k, loss):
        at_ = pl.ds(pl.multiple_of(k * CG, CG), CG)
        corr_ = C[at_, :] / B
        row_ids = row0 + k * CG + lax.broadcasted_iota(jnp.int32, (CG, T), 0)
        col_ids = col0 + lax.broadcasted_iota(jnp.int32, (CG, T), 1)
        on = row_ids == col_ids
        miss = 1.0 - corr_
        loss = loss + fold8(jnp.where(on, miss * miss, off_weight * corr_ * corr_))
        g = (jnp.where(on, -2.0 * miss, 2.0 * off_weight * corr_) * scale).astype(bf16)
        G[at_, :] = g
        prod = g.astype(f32) * corr_
        high = prod.astype(bf16)
        GH[at_, :] = high
        GL[at_, :] = (prod - high.astype(f32)).astype(bf16)
        return loss

    loss = lax.fori_loop(0, T // CG, grad, jnp.zeros((8, T), f32))
    loss_tile = loss[:, 0:128]
    for k in range(128, T, 128):
        loss_tile = loss_tile + loss[:, k : k + 128]

    def p2(i, u):
        return dot_nn(V1[pl.ds(pl.multiple_of(i * R + PIECES[u][0], 16), PIECES[u][1]), :], G[...])

    def p1(i):
        return dot_nt(V2[rows(i), :], G[...])

    def arrived(key, u):
        slot = ZSLOT[key]
        recv(("s", key, u), part(zr, slot, u))
        return part(zr, slot, u)[...].astype(f32)

    def zc(r, k, over_y=False, take=()):
        key = ("y", k) if over_y else (r, k)
        dev = to_yh if over_y else to["m"] if k > 0 else to["p"]
        for u in range(len(PIECES)):
            val = p2(fti(r, -k), u)
            for source in take:
                val = val + arrived(source, u)
            part(zs, ZSLOT[key], u)[...] = val.astype(bf16)
            send(("s", key, u), part(zs, ZSLOT[key], u), part(zr, ZSLOT[key], u), dev)

    def z_end():
        for u in range(len(PIECES)):
            val = p2(fti(0, 0), u)
            for source in ((0, 1), (0, -1), ("y", 0)):
                val = val + arrived(source, u)
            U2[pl.ds(*PIECES[u]), :] = val

    def core_send(r, dx):
        slot = CSLOT[r, dx]
        cs[slot] = p1(dpi(r, dx, 1)).astype(bf16)
        send(("s", "c", r, dx), cs.at[slot], cr.at[slot], to_core)

    def both(r, dx):
        dx = dx % NX
        val = p1(dpi(r, dx))
        slot = CSLOT[r, dx]
        recv(("s", "c", r, dx), cr.at[slot])
        return val + cr[slot].astype(f32)

    def xc(d, r, s):
        val = both(r, SIGN[d] * (KX[d, r] - s))
        if s:
            prev = XSLOT[d, r, s - 1]
            recv(("s", d, r, s - 1), xr.at[prev])
            val = val + xr[prev].astype(f32)
        slot = XSLOT[d, r, s]
        xs[slot] = val.astype(bf16)
        send(("s", d, r, s), xs.at[slot], xr.at[slot], to[d])

    def x_end(r):
        val = both(r, 0)
        for d in ("xp", "xm"):
            last = KX[d, r] - 1
            slot = XSLOT[d, r, last]
            recv(("s", d, r, last), xr.at[slot])
            val = val + xr[slot].astype(f32)
        return val

    zc(1, 4)
    zc(1, -3)
    zc(1, 1, True)
    zc(1, 0, True)
    for r, dx in CORDER:
        core_send(r, dx)
    zc(0, 4)
    zc(0, -3)

    ones = jnp.ones((16, T), bf16)
    second1 = dot_nt(ones, GH[...]) + dot_nt(ones, GL[...])
    second2 = dot_nn(ones, GH[...]) + dot_nn(ones, GL[...])
    lane_row = lax.broadcasted_iota(jnp.int32, (16, T), 0)

    def split_rows(M):
        s = jnp.concatenate([M[24:32, :], M[24:32, :]], axis=0)
        high = s.astype(bf16).astype(f32)
        low = s - high
        return jnp.where(lane_row == 0, high, jnp.where(lane_row == 1, low, 0.0)).astype(bf16)

    first1 = jnp.sum(dot_nt(split_rows(M2), G[...]), axis=0, keepdims=True) / B
    first2 = jnp.sum(dot_nn(split_rows(M1), G[...]), axis=0, keepdims=True) / B
    top = lane_row[0:8] == 0
    A1[0, :, 0:T] = jnp.where(top, jnp.broadcast_to(first1, (8, T)), second1[0:8])
    A1[0, :, T : T + 128] = loss_tile
    A2[0] = jnp.where(top, jnp.broadcast_to(first2, (8, T)), second2[0:8])

    def put(n):
        send(("a1", n), A1.at[n], R1.at[n], dp_steps[n])
        send(("a2", n), A2.at[n], R2.at[n], feat_steps[n])

    def take(n):
        recv(("a1", n), R1.at[n])
        recv(("a2", n), R2.at[n])
        A1[n + 1] = A1[n] + R1[n]
        A2[n + 1] = A2[n] + R2[n]

    put(0)
    xc("xp", 0, 0)
    xc("xm", 1, 0)
    zc(1, 3, take=[(1, 4)])
    zc(1, -2, take=[(1, -3)])
    take(0)
    put(1)
    xc("xp", 1, 0)
    xc("xm", 0, 0)
    zc(0, 3, take=[(0, 4)])
    zc(0, -2, take=[(0, -3)])
    zc(1, 2, True, take=[(1, 3)])
    zc(1, -1, True, take=[(1, -2)])
    take(1)
    put(2)
    xc("xp", 0, 1)
    xc("xm", 1, 1)
    take(2)
    put(3)
    ys[0] = x_end(1).astype(bf16)
    send(("s", "yl"), ys.at[0], yr.at[0], to_yl)
    take(3)
    zc(0, 2, take=[(0, 3), ("y", 2)])
    zc(0, -1, take=[(0, -2), ("y", -1)])

    def delta(U, V, M, A, D, i):
        stats = A[4]
        first = stats[0:1, 0:T] / B
        second = stats[1:2, 0:T] / B
        inv = M[16:17, :]

        def body(k, carry):
            off = pl.multiple_of(k * CH, 16)
            at_ = pl.ds(pl.multiple_of(i * R + k * CH, 16), CH)
            own = V[at_, :].astype(f32)
            D[at_, :] = (inv * (U[pl.ds(off, CH), :] / B - first - own * second)).astype(bf16)
            return carry

        lax.fori_loop(0, R // CH, body, 0)

    val = x_end(0)
    recv(("s", "yl"), yr.at[0])
    U1[...] = val + yr[0].astype(f32)
    delta(U1, V1, M1, A1, D1, dp)
    start_a("d", D1, at(D1, dp))
    zc(0, 1, take=[(0, 2), ("y", 1)])

    AL[0] = A1[4, :, T : T + 128]

    def put_l(n):
        send(("al", n), AL.at[n], RL.at[n], feat_steps[n])

    def take_l(n):
        recv(("al", n), RL.at[n])
        AL[n + 1] = AL[n] + RL[n]

    put_l(0)
    take_l(0)
    put_l(1)
    z_end()
    delta(U2, V2, M2, A2, D2, ft)
    start_b("d", D2, at(D2, ft))

    local[2].wait()
    local[3].wait()

    def weight(w_ref, X, D, i, first=False):
        term = dot_tn(X[rows(i), :], D[rows(i), :])
        if first:
            w_ref[...] = term
        else:
            w_ref[...] += term

    def weights_one():
        w1_ref[...] = dot_tn(X1[0:KC, :], D1[0:KC, :])

        def body(k, carry):
            at_ = pl.ds(pl.multiple_of(k * KC, 16), KC)
            w1_ref[...] += dot_tn(X1[at_, :], D1[at_, :])
            return carry

        lax.fori_loop(1, B // KC, body, 0)

    def loss_step(n):
        def step():
            take_l(n)
            if n < 3:
                put_l(n + 1)
            else:
                loss_ref[0] = jnp.sum(AL[4]) / F

        return (step,)

    weight(w2_ref, X2, D2, ft, True)
    order = (
        ORDER[: 2 * NP] + [loss_step(1)] + ORDER[2 * NP : 4 * NP + 3] + [loss_step(2)]
        + ORDER[4 * NP + 3 : NORM] + [(weights_one,)] + ORDER[NORM : NORM + NP]
        + [loss_step(3)] + ORDER[NORM + NP :]
    )
    gather(order, "d", D1, D2, lambda i: None, lambda i: weight(w2_ref, X2, D2, i))
    drain()
    assert len(names) <= NSEM


def per_device(view_one, view_two, inputs_one, inputs_two, loss_scale):
    R, T = view_one.shape
    B = inputs_one.shape[0]
    block = (R, T)
    anywhere = pl.BlockSpec(memory_space=pl.ANY)
    vmem = pl.BlockSpec(memory_space=pltpu.VMEM)
    smem = pl.BlockSpec(memory_space=pltpu.SMEM)
    V = pltpu.VMEM
    scratch = [
        V((B, T), bf16), V((B, T), bf16), V((B, T), bf16), V((B, T), bf16),
        V((B, T), bf16), V((B, T), bf16),
        V((len(ZSLOT),) + block, bf16), V((len(ZSLOT),) + block, bf16),
        V((len(CSLOT),) + block, bf16), V((len(CSLOT),) + block, bf16),
        V((len(XSLOT),) + block, bf16), V((len(XSLOT),) + block, bf16),
        V((1,) + block, bf16), V((1,) + block, bf16),
        V(block, f32), V(block, f32),
        V((T, T), f32), V((T, T), bf16), V((T, T), bf16), V((T, T), bf16),
        V((32, T), f32), V((32, T), f32),
        V((5, 8, T + 128), f32), V((4, 8, T + 128), f32),
        V((5, 8, T), f32), V((4, 8, T), f32),
        V((5, 8, 128), f32), V((4, 8, 128), f32),
        pltpu.SemaphoreType.DMA((NSEM,)),
        pltpu.SemaphoreType.DMA((NSEM,)),
        pltpu.SemaphoreType.DMA((4,)),
    ]
    return pl.pallas_call(
        kernel,
        out_shape=(
            jax.ShapeDtypeStruct((1,), f32),
            V((T, T), f32),
            V((T, T), f32),
        ),
        in_specs=[anywhere] * 4 + [smem],
        out_specs=(smem, vmem, vmem),
        scratch_shapes=scratch,
        compiler_params=pltpu.CompilerParams(
            collective_id=0, has_side_effects=True, vmem_limit_bytes=58 * 1024 * 1024
        ),
        cost_estimate=pl.CostEstimate(
            flops=10 * B * T * T, bytes_accessed=4 * B * T + 8 * T * T, transcendentals=0
        ),
    )(view_one, view_two, inputs_one, inputs_two, loss_scale)


def solution(mesh):
    placed = (P("dp", "feat"), P("feat", "dp"), P(None, "dp"), P(None, "feat"), P())
    return jax.shard_map(
        per_device,
        mesh=mesh,
        in_specs=placed,
        out_specs=(P(), P("dp", "feat"), P("feat", "dp")),
        check_vma=False,
    )
```

```python
import jax
import jax.numpy as jnp
from jax import lax
from jax.experimental import pallas as pl
from jax.experimental.pallas import tpu as pltpu
from jax.sharding import PartitionSpec as P

F = 8192
off_weight = 0.0051
epsilon = 1e-05
MESH = pl.DeviceIdType.MESH
f32 = jnp.float32
bf16 = jnp.bfloat16

NX = 4
NZ = 8
SIGN = {"xp": 1, "xm": -1}
KX = {("xp", 0): 2, ("xm", 0): 1, ("xp", 1): 1, ("xm", 1): 2}
PIECES = ((0, 128), (128, 112))
NP = len(PIECES)
ZSLOT = {
    key: n
    for n, key in enumerate(
        [(1, 4), (1, 3), (1, -3), (1, -2), (0, 4), (0, 3), (0, 2), (0, 1), (0, -3), (0, -2), (0, -1)]
        + [("y", 2), ("y", -1), ("y", 1), ("y", 0)]
    )
}
XSLOT = {}
for key, hops in KX.items():
    for hop in range(hops):
        XSLOT[key + (hop,)] = len(XSLOT)
CORDER = [(0, 2), (1, 2), (1, 1), (0, 3), (0, 1), (1, 3), (1, 0), (0, 0)]
CSLOT = {key: n for n, key in enumerate(CORDER)}
NSEM = 240

def both_z(r, hp, hm):
    return [("z", d, r, h, u) for u in range(NP) for d, h in (("p", hp), ("m", hm)) if h]


def one_z(d, r, h):
    return [("z", d, r, h, u) for u in range(NP)]


def over_y(d, h):
    return [("y", d, h, u) for u in range(NP)]


ORDER = [
    both_z(0, 1, 1),
    [("yl",), ("x", "xp", 0, 1), ("x", "xm", 0, 1)],
    both_z(0, 2, 2),
    [("x", "xp", 1, 1), ("x", "xm", 1, 1)] + over_y("m", 1) + [("ls", 0)],
    both_z(0, 3, 3),
    [("x", "xp", 0, 2), ("x", "xm", 1, 2)] + over_y("p", 2) + [("ls", 1)],
    one_z("m", 1, 2),
    [("c", r, dx) for r, dx in CORDER],
    one_z("p", 0, 4),
    one_z("p", 1, 3),
    one_z("m", 1, 3),
    [("lr", 0), ("lr", 1)],
    one_z("p", 1, 4),
]
WHOLE = 7


def dot_tn(left, right):
    return lax.dot_general(left, right, (((0,), (0,)), ((), ())), preferred_element_type=f32)


def dot_nt(left, right):
    return lax.dot_general(left, right, (((1,), (1,)), ((), ())), preferred_element_type=f32)


def dot_nn(left, right):
    return lax.dot_general(left, right, (((1,), (0,)), ((), ())), preferred_element_type=f32)


def fold8(block):
    total = block[0:8]
    for k in range(8, block.shape[0], 8):
        total = total + block[k : k + 8]
    return total


def kernel(
    view1, view2, in1, in2, scale_ref,
    loss_ref, w1_ref, w2_ref,
    V1, V2, D1, D2, X1, X2, P1, P2, PT,
    zs, zr, cs, cr, xs, xr, ys, yr, U1, U2,
    C, G, GH, GL, M1, M2, A1, R1, A2, R2, AL, RL,
    ssem, rsem, lsem,
):
    R = view1.shape[0]
    B = V1.shape[0]
    T = V1.shape[1]
    dp = lax.axis_index("dp")
    ft = lax.axis_index("feat")
    c = lax.rem(dp, 2)
    x = lax.rem(lax.div(dp, 2), NX)
    yl = lax.div(dp, 2 * NX)
    yh = lax.rem(ft, 2)
    z = lax.div(ft, 2)

    def dpi(r, dx, other=0):
        y_ = yl if r == 0 else 1 - yl
        c_ = 1 - c if other else c
        return (y_ * NX + lax.rem(x + (dx % NX), NX)) * 2 + c_

    turn = 1 - 2 * c

    def fti(r, dz):
        y_ = yh if r == 0 else 1 - yh
        return lax.rem(z + NZ + dz * turn, NZ) * 2 + y_

    def rows(i):
        return pl.ds(pl.multiple_of(i * R, 16), R)

    def at(buf, i, u=None):
        if u is None:
            return buf.at[rows(i)]
        return buf.at[pl.ds(pl.multiple_of(i * R + PIECES[u][0], 16), PIECES[u][1])]

    def part(buf, slot, u):
        return buf.at[slot, pl.ds(*PIECES[u])]

    to_core = {"dp": dpi(0, 0, 1), "feat": ft}
    to_yl = {"dp": dpi(1, 0), "feat": ft}
    to_yh = {"dp": dp, "feat": fti(1, 0)}
    to = {
        "xp": {"dp": dpi(0, 1), "feat": ft},
        "xm": {"dp": dpi(0, -1), "feat": ft},
        "p": {"dp": dp, "feat": fti(0, 1)},
        "m": {"dp": dp, "feat": fti(0, -1)},
    }
    xa = x + 1 - 2 * lax.rem(x, 2)
    xb = NX - 1 - x
    za = z + 1 - 2 * lax.rem(z, 2)
    zb = z + 2 - 4 * lax.rem(lax.div(z, 2), 2)
    dp_steps = [
        to_core,
        to_yl,
        {"dp": (yl * NX + xa) * 2 + c, "feat": ft},
        {"dp": (yl * NX + xb) * 2 + c, "feat": ft},
    ]
    to_zb = {"dp": dp, "feat": zb * 2 + yh}
    to_zc = {"dp": dp, "feat": fti(0, 4)}
    feat_steps = [to_yh, {"dp": dp, "feat": za * 2 + yh}, to_zb, to_zc]

    peers = [to_core, to_yl, to_yh, to["xp"], to["xm"], to["p"], to["m"], to_zb, to_zc]
    barrier = pltpu.get_barrier_semaphore()
    for peer in peers:
        pl.semaphore_signal(barrier, inc=1, device_id=peer, device_id_type=MESH)
    local = [
        pltpu.make_async_copy(view1, at(V1, dp), lsem.at[0]),
        pltpu.make_async_copy(view2, at(V2, ft), lsem.at[1]),
        pltpu.make_async_copy(in1, X1, lsem.at[2]),
        pltpu.make_async_copy(in2, X2, lsem.at[3]),
    ]
    for copy in local:
        copy.start()
    pl.semaphore_wait(barrier, len(peers))

    names = {}
    flying = {}

    def index(name):
        return names.setdefault(name, len(names))

    def send(name, src, dst, dev):
        k = index(name)
        copy = pltpu.make_async_remote_copy(
            src_ref=src, dst_ref=dst, send_sem=ssem.at[k], recv_sem=rsem.at[k],
            device_id=dev, device_id_type=MESH,
        )
        copy.start()
        flying[name] = copy

    def recv(name, dst):
        k = index(name)
        pltpu.make_async_remote_copy(
            src_ref=dst, dst_ref=dst, send_sem=ssem.at[k], recv_sem=rsem.at[k],
            device_id=to_core, device_id_type=MESH,
        ).wait_recv()

    def drain(keep=lambda name: True):
        for name in [n for n in flying if keep(n)]:
            flying.pop(name).wait_send()

    def start_a(tag, A, src):
        own = at(A, dp)
        send((tag, "yl"), src, own, to_yl)
        send((tag, "xp", 0, 1), src, own, to["xp"])
        send((tag, "xm", 0, 1), src, own, to["xm"])
        send((tag, "c", 0, 0), src, own, to_core)

    def start_b(tag, Bb, src, u):
        for d in ("p", "m"):
            send((tag, d, 0, 1, u), src.at[pl.ds(*PIECES[u])], at(Bb, ft, u), to[d])

    def ev_yl(tag, A):
        i = dpi(1, 0)
        recv((tag, "yl"), at(A, i))
        send((tag, "xp", 1, 1), at(A, i), at(A, i), to["xp"])
        send((tag, "xm", 1, 1), at(A, i), at(A, i), to["xm"])
        send((tag, "c", 1, 0), at(A, i), at(A, i), to_core)
        return i

    def ev_z(tag, Bb, d, r, h, u):
        i = fti(r, -h if d == "p" else h)
        piece = at(Bb, i, u)
        recv((tag, d, r, h, u), piece)
        if r == 0 and (d, h) in (("m", 1), ("p", 2)):
            send((tag, "y", d, h, u), piece, piece, to_yh)
        if h < (4 if d == "p" else 3):
            send((tag, d, r, h + 1, u), piece, piece, to[d])
        return i

    def ev_y(tag, Bb, d, h, u):
        i = fti(1, -h if d == "p" else h)
        piece = at(Bb, i, u)
        recv((tag, "y", d, h, u), piece)
        send((tag, d, 1, h + 1, u), piece, piece, to[d])
        return i

    def ev_x(tag, A, d, r, h):
        dx = (-SIGN[d] * h) % NX
        i = dpi(r, dx)
        recv((tag, d, r, h), at(A, i))
        if h < KX[d, r]:
            send((tag, d, r, h + 1), at(A, i), at(A, i), to[d])
        send((tag, "c", r, dx), at(A, i), at(A, i), to_core)
        return i

    def late_send(tag, Bb, n):
        block = at(Bb, fti(0, -n))
        send((tag, "y", n), block, block, to_yh)

    def late_recv(tag, Bb, n):
        i = fti(1, -n)
        recv((tag, "y", n), at(Bb, i))
        return i

    def gather(tag, A, Bb, hook_a, hook_b, after):
        last = len(PIECES) - 1
        for n, group in enumerate(ORDER):
            work = []
            for kind, *args in group:
                if kind == "z" or kind == "y":
                    i = (ev_z if kind == "z" else ev_y)(tag, Bb, *args)
                    if args[-1] == last:
                        work.append((hook_b, i))
                elif kind == "ls":
                    late_send(tag, Bb, *args)
                elif kind == "lr":
                    work.append((hook_b, late_recv(tag, Bb, *args)))
                elif kind == "yl":
                    work.append((hook_a, ev_yl(tag, A)))
                elif kind == "x":
                    work.append((hook_a, ev_x(tag, A, *args)))
                else:
                    work.append((hook_a, ev_c(tag, A, *args)))
            for hook, i in work:
                hook(i)
            if n in after:
                after[n]()

    def ev_c(tag, A, r, dx):
        i = dpi(r, dx, 1)
        recv((tag, "c", r, dx), at(A, i))
        return i

    CH = 48

    def moments(V, M, i):
        base = i * R

        def body(k, carry):
            s, q = carry
            v = V[pl.ds(pl.multiple_of(base + k * CH, 16), CH), :].astype(f32)
            return s + fold8(v), q + fold8(v * v)

        s, q = lax.fori_loop(0, R // CH, body, (M[0:8, :], M[8:16, :]))
        M[0:8, :] = s
        M[8:16, :] = q

    def statistics(M):
        average = jnp.sum(M[0:8, :], axis=0, keepdims=True) / B
        spread = jnp.sum(M[8:16, :], axis=0, keepdims=True) / B - average * average
        M[16:24, :] = jnp.broadcast_to(lax.rsqrt(spread + epsilon), (8, T))
        M[32:40, :] = jnp.broadcast_to(average, (8, T))

    def normalize(V, M):
        average = M[32:33, :]
        inv = M[16:17, :]

        def body(k, total):
            at_ = pl.ds(pl.multiple_of(k * CH, 16), CH)
            n = ((V[at_, :].astype(f32) - average) * inv).astype(bf16)
            V[at_, :] = n
            return total + fold8(n.astype(f32))

        total = lax.fori_loop(0, B // CH, body, jnp.zeros((8, T), f32))
        M[24:32, :] = jnp.broadcast_to(jnp.sum(total, axis=0, keepdims=True), (8, T))

    M1[...] = jnp.zeros_like(M1)
    M2[...] = jnp.zeros_like(M2)
    for u in range(NP):
        start_b("g", V2, view2, u)
    start_a("g", V1, view1)
    local[0].wait()
    local[1].wait()
    moments(V1, M1, dp)
    moments(V2, M2, ft)

    ready = []
    waiting = [ft]

    def corr(i):
        C[...] += dot_tn(V1[rows(i), :], V2[rows(i), :])

    def work_two(i):
        moments(V2, M2, i)
        if ready:
            corr(i)
        else:
            waiting.append(i)

    def some(count):
        for _ in range(min(count, len(waiting))):
            corr(waiting.pop(0))

    def first_whole():
        drain(lambda n: n[1] in ("c", "xp", "xm", "yl"))
        statistics(M1)
        normalize(V1, M1)
        C[...] = jnp.zeros_like(C)
        ready.append(True)
        some(4)

    after = {WHOLE: first_whole, WHOLE + 1: lambda: some(2), WHOLE + 2: lambda: some(4), WHOLE + 3: lambda: some(20)}
    gather("g", V1, V2, lambda i: moments(V1, M1, i), work_two, after)
    statistics(M2)

    KC = 768
    lane_row = lax.broadcasted_iota(jnp.int32, (16, T), 0)

    def split(value):
        high = value.astype(bf16).astype(f32)
        return high, value - high

    s_high, s_low = split(jnp.concatenate([M1[24:32, :], M1[24:32, :]], axis=0))
    a_high, a_low = split(jnp.concatenate([M2[32:40, :], M2[32:40, :]], axis=0))
    left = jnp.where(lane_row < 2, s_high, jnp.where(lane_row < 4, s_low, 0.0)).astype(bf16)
    right = jnp.where(lane_row % 2 == 0, a_high, a_low).astype(bf16)
    C[...] -= dot_tn(left, right)

    CG = 32
    scale = scale_ref[0]
    inv_two = M2[16:17, :] / B
    row0 = ft * T
    col0 = dp * T

    def grad(k, loss):
        at_ = pl.ds(pl.multiple_of(k * CG, CG), CG)
        corr_ = C[at_, :] * inv_two
        row_ids = row0 + k * CG + lax.broadcasted_iota(jnp.int32, (CG, T), 0)
        col_ids = col0 + lax.broadcasted_iota(jnp.int32, (CG, T), 1)
        on = row_ids == col_ids
        miss = 1.0 - corr_
        loss = loss + fold8(jnp.where(on, miss * miss, off_weight * corr_ * corr_))
        g = (jnp.where(on, -2.0 * miss, 2.0 * off_weight * corr_) * scale).astype(bf16)
        G[at_, :] = g
        prod = g.astype(f32) * corr_
        high = prod.astype(bf16)
        GH[at_, :] = high
        GL[at_, :] = (prod - high.astype(f32)).astype(bf16)
        return loss

    loss = lax.fori_loop(0, T // CG, grad, jnp.zeros((8, T), f32))
    loss_tile = loss[:, 0:128]
    for k in range(128, T, 128):
        loss_tile = loss_tile + loss[:, k : k + 128]

    DC = 16

    def delta(U, V, M, A, D, i, start, count):
        stats = A[4]
        first = stats[0:1, 0:T] / B
        second = stats[1:2, 0:T] / B
        inv = M[16:17, :]

        def body(k, carry):
            off = pl.multiple_of(start + k * DC, 16)
            at_ = pl.ds(pl.multiple_of(i * R + start + k * DC, 16), DC)
            own = V[at_, :].astype(f32)
            D[at_, :] = (inv * (U[pl.ds(off, DC), :] / B - first - own * second)).astype(bf16)
            return carry

        lax.fori_loop(0, count // DC, body, 0)

    def pair2(dz):
        at_ = pl.ds(pl.multiple_of(fti(0, dz) // 2 * (2 * R), 16), 2 * R)
        P2[at_, :] = dot_nn(V1[at_, :], G[...])

    def pair1(r, dx):
        PT[...] = dot_nt(V2[pl.ds(pl.multiple_of(dpi(r, dx) // 2 * (2 * R), 16), 2 * R), :], G[...])
        P1[CSLOT[r, dx]] = PT[rows(c), :]

    def p2(i, u):
        return P2[pl.ds(pl.multiple_of(i * R + PIECES[u][0], 16), PIECES[u][1]), :]

    def arrived(key, u):
        slot = ZSLOT[key]
        recv(("s", key, u), part(zr, slot, u))
        return part(zr, slot, u)[...].astype(f32)

    def zc(u, r, k, over_y=False, take=()):
        key = ("y", k) if over_y else (r, k)
        dev = to_yh if over_y else to["m"] if k > 0 else to["p"]
        val = p2(fti(r, -k), u)
        for source in take:
            val = val + arrived(source, u)
        part(zs, ZSLOT[key], u)[...] = val.astype(bf16)
        send(("s", key, u), part(zs, ZSLOT[key], u), part(zr, ZSLOT[key], u), dev)

    def z_end(u):
        val = p2(fti(0, 0), u)
        for source in ((0, 1), (0, -1), ("y", 0)):
            val = val + arrived(source, u)
        U2[pl.ds(*PIECES[u]), :] = val
        delta(U2, V2, M2, A2, D2, ft, *PIECES[u])
        start_b("d", D2, at(D2, ft), u)

    def far(u):
        if u == 0:
            pair2(-4)
            pair2(3)
        zc(u, 1, 4)
        zc(u, 1, -3)

    def far_own(u):
        zc(u, 0, 4)
        zc(u, 0, -3)

    def middle(u):
        if u == 0:
            pair2(-3)
            pair2(2)
        zc(u, 1, 3, take=[(1, 4)])
        zc(u, 1, -2, take=[(1, -3)])

    def middle_own(u):
        zc(u, 0, 3, take=[(0, 4)])
        zc(u, 0, -2, take=[(0, -3)])

    def cross(u):
        if u == 0:
            pair2(-2)
            pair2(1)
        zc(u, 1, 2, True, take=[(1, 3)])
        zc(u, 1, -1, True, take=[(1, -2)])

    def near(u):
        zc(u, 0, 2, take=[(0, 3), ("y", 2)])
        zc(u, 0, -1, take=[(0, -2), ("y", -1)])

    def nearest(u):
        zc(u, 0, 1, take=[(0, 2), ("y", 1)])

    def core_send(r, dx):
        pair1(r, dx)
        slot = CSLOT[r, dx]
        cs[slot] = PT[rows(1 - c), :].astype(bf16)
        send(("s", "c", r, dx), cs.at[slot], cr.at[slot], to_core)

    def both(r, dx):
        dx = dx % NX
        slot = CSLOT[r, dx]
        val = P1[slot]
        recv(("s", "c", r, dx), cr.at[slot])
        return val + cr[slot].astype(f32)

    def xc(d, r, s):
        val = both(r, SIGN[d] * (KX[d, r] - s))
        if s:
            prev = XSLOT[d, r, s - 1]
            recv(("s", d, r, s - 1), xr.at[prev])
            val = val + xr[prev].astype(f32)
        slot = XSLOT[d, r, s]
        xs[slot] = val.astype(bf16)
        send(("s", d, r, s), xs.at[slot], xr.at[slot], to[d])

    def x_end(r):
        val = both(r, 0)
        for d in ("xp", "xm"):
            last = KX[d, r] - 1
            slot = XSLOT[d, r, last]
            recv(("s", d, r, last), xr.at[slot])
            val = val + xr[slot].astype(f32)
        return val

    far(0)
    far(1)
    drain(lambda n: n[0] == "g")
    normalize(V2, M2)
    pair2(-1)
    zc(0, 1, 1, True)
    zc(1, 1, 1, True)
    for r, dx in CORDER[0:4]:
        core_send(r, dx)
    middle(0)
    far_own(0)
    xc("xp", 0, 0)
    xc("xm", 1, 0)
    middle(1)
    for r, dx in CORDER[4:8]:
        core_send(r, dx)
    far_own(1)

    ones = jnp.ones((16, T), bf16)
    second1 = dot_nt(ones, GH[...]) + dot_nt(ones, GL[...])
    second2 = dot_nn(ones, GH[...]) + dot_nn(ones, GL[...])

    def split_rows(M):
        s = jnp.concatenate([M[24:32, :], M[24:32, :]], axis=0)
        high = s.astype(bf16).astype(f32)
        low = s - high
        return jnp.where(lane_row == 0, high, jnp.where(lane_row == 1, low, 0.0)).astype(bf16)

    first1 = jnp.sum(dot_nt(split_rows(M2), G[...]), axis=0, keepdims=True) / B
    first2 = jnp.sum(dot_nn(split_rows(M1), G[...]), axis=0, keepdims=True) / B
    top = lane_row[0:8] == 0
    A1[0, :, 0:T] = jnp.where(top, jnp.broadcast_to(first1, (8, T)), second1[0:8])
    A1[0, :, T : T + 128] = loss_tile
    A2[0] = jnp.where(top, jnp.broadcast_to(first2, (8, T)), second2[0:8])

    def put(n):
        send(("a1", n), A1.at[n], R1.at[n], dp_steps[n])
        send(("a2", n), A2.at[n], R2.at[n], feat_steps[n])

    def take(n):
        recv(("a1", n), R1.at[n])
        recv(("a2", n), R2.at[n])
        A1[n + 1] = A1[n] + R1[n]
        A2[n + 1] = A2[n] + R2[n]

    put(0)
    cross(0)
    xc("xp", 1, 0)
    xc("xm", 0, 0)
    middle_own(0)
    take(0)
    put(1)
    cross(1)
    middle_own(1)
    xc("xp", 0, 1)
    xc("xm", 1, 1)
    take(1)
    put(2)
    pair2(0)
    zc(0, 1, 0, True)
    zc(1, 1, 0, True)
    near(0)
    take(2)
    put(3)
    ys[0] = x_end(1).astype(bf16)
    send(("s", "yl"), ys.at[0], yr.at[0], to_yl)
    near(1)
    take(3)
    nearest(0)
    val = x_end(0)
    recv(("s", "yl"), yr.at[0])
    U1[...] = val + yr[0].astype(f32)
    delta(U1, V1, M1, A1, D1, dp, 0, R)
    start_a("d", D1, at(D1, dp))
    AL[0] = A1[4, :, T : T + 128]

    def put_l(n):
        send(("al", n), AL.at[n], RL.at[n], feat_steps[n])

    def take_l(n):
        recv(("al", n), RL.at[n])
        AL[n + 1] = AL[n] + RL[n]

    put_l(0)
    nearest(1)
    z_end(0)
    take_l(0)
    put_l(1)
    z_end(1)
    local[2].wait()
    local[3].wait()

    def weight(w_ref, X, D, i, first=False):
        term = dot_tn(X[rows(i), :], D[rows(i), :])
        if first:
            w_ref[...] = term
        else:
            w_ref[...] += term

    def weights_one():
        w1_ref[...] = dot_tn(X1[0:KC, :], D1[0:KC, :])

        def body(k, carry):
            at_ = pl.ds(pl.multiple_of(k * KC, 16), KC)
            w1_ref[...] += dot_tn(X1[at_, :], D1[at_, :])
            return carry

        lax.fori_loop(1, B // KC, body, 0)

    def loss_step(n):
        take_l(n)
        if n < 3:
            put_l(n + 1)
        else:
            loss_ref[0] = jnp.sum(AL[4]) / F

    weight(w2_ref, X2, D2, ft, True)
    after = {0: lambda: loss_step(1), 2: lambda: loss_step(2), 4: lambda: loss_step(3), WHOLE: weights_one}
    gather("d", D1, D2, lambda i: None, lambda i: weight(w2_ref, X2, D2, i), after)
    drain()
    assert len(names) <= NSEM


def per_device(view_one, view_two, inputs_one, inputs_two, loss_scale):
    R, T = view_one.shape
    B = inputs_one.shape[0]
    block = (R, T)
    anywhere = pl.BlockSpec(memory_space=pl.ANY)
    vmem = pl.BlockSpec(memory_space=pltpu.VMEM)
    smem = pl.BlockSpec(memory_space=pltpu.SMEM)
    V = pltpu.VMEM
    scratch = [
        V((B, T), bf16), V((B, T), bf16), V((B, T), bf16), V((B, T), bf16),
        V((B, T), bf16), V((B, T), bf16), V((len(CSLOT),) + block, f32), V((B, T), f32), V((2 * R, T), f32),
        V((len(ZSLOT),) + block, bf16), V((len(ZSLOT),) + block, bf16),
        V((len(CSLOT),) + block, bf16), V((len(CSLOT),) + block, bf16),
        V((len(XSLOT),) + block, bf16), V((len(XSLOT),) + block, bf16),
        V((1,) + block, bf16), V((1,) + block, bf16),
        V(block, f32), V(block, f32),
        V((T, T), f32), V((T, T), bf16), V((T, T), bf16), V((T, T), bf16),
        V((40, T), f32), V((40, T), f32),
        V((5, 8, T + 128), f32), V((4, 8, T + 128), f32),
        V((5, 8, T), f32), V((4, 8, T), f32),
        V((5, 8, 128), f32), V((4, 8, 128), f32),
        pltpu.SemaphoreType.DMA((NSEM,)),
        pltpu.SemaphoreType.DMA((NSEM,)),
        pltpu.SemaphoreType.DMA((4,)),
    ]
    return pl.pallas_call(
        kernel,
        out_shape=(
            jax.ShapeDtypeStruct((1,), f32),
            V((T, T), f32),
            V((T, T), f32),
        ),
        in_specs=[anywhere] * 4 + [smem],
        out_specs=(smem, vmem, vmem),
        scratch_shapes=scratch,
        compiler_params=pltpu.CompilerParams(
            collective_id=0, has_side_effects=True, vmem_limit_bytes=59 * 1024 * 1024
        ),
        cost_estimate=pl.CostEstimate(
            flops=10 * B * T * T, bytes_accessed=4 * B * T + 8 * T * T, transcendentals=0
        ),
    )(view_one, view_two, inputs_one, inputs_two, loss_scale)


def solution(mesh):
    placed = (P("dp", "feat"), P("feat", "dp"), P(None, "dp"), P(None, "feat"), P())
    return jax.shard_map(
        per_device,
        mesh=mesh,
        in_specs=placed,
        out_specs=(P(), P("dp", "feat"), P("feat", "dp")),
        check_vma=False,
    )
```

```python
import jax
import jax.numpy as jnp
from jax import lax
from jax.experimental import pallas as pl
from jax.experimental.pallas import tpu as pltpu
from jax.sharding import PartitionSpec as P

F = 8192
off_weight = 0.0051
epsilon = 1e-05
MESH = pl.DeviceIdType.MESH
f32 = jnp.float32
bf16 = jnp.bfloat16

NX = 4
NZ = 8
SIGN = {"xp": 1, "xm": -1}
KX = {("xp", 0): 2, ("xm", 0): 1, ("xp", 1): 1, ("xm", 1): 2}
PIECES = ((0, 128), (128, 112))
NP = len(PIECES)
ZSLOT = {
    key: n
    for n, key in enumerate(
        [(1, 4), (1, 3), (1, -3), (1, -2), (0, 4), (0, 3), (0, 2), (0, 1), (0, -3), (0, -2), (0, -1)]
        + [("y", 2), ("y", -1), ("y", 1), ("y", 0)]
    )
}
XSLOT = {}
for key, hops in KX.items():
    for hop in range(hops):
        XSLOT[key + (hop,)] = len(XSLOT)
CORDER = [(0, 2), (1, 2), (1, 1), (0, 3), (0, 1), (1, 3), (1, 0), (0, 0)]
CSLOT = {key: n for n, key in enumerate(CORDER)}
NSEM = 83
FINAL = (("p", 0, 4), ("m", 0, 3), ("m", 1, 3))

def both_z(r, hp, hm):
    return [("z", d, r, h, u) for u in range(NP) for d, h in (("p", hp), ("m", hm)) if h]


def one_z(d, r, h):
    return [("z", d, r, h, u) for u in range(NP)]


def over_y(d, h):
    return [("y", d, h, u) for u in range(NP)]


ORDER = [
    both_z(0, 1, 1),
    [("yl",), ("x", "xp", 0, 1), ("x", "xm", 0, 1)],
    both_z(0, 2, 2),
    [("x", "xp", 1, 1), ("x", "xm", 1, 1)] + over_y("m", 1) + [("ls", 0)],
    both_z(0, 3, 3),
    [("x", "xp", 0, 2), ("x", "xm", 1, 2)] + over_y("p", 2) + [("ls", 1)],
    one_z("m", 1, 2),
    [("c",)],
    one_z("p", 0, 4),
    one_z("p", 1, 3),
    one_z("m", 1, 3),
    [("lr",)],
    one_z("p", 1, 4),
]
WHOLE = 7


def dot_tn(left, right):
    return lax.dot_general(left, right, (((0,), (0,)), ((), ())), preferred_element_type=f32)


def dot_nt(left, right):
    return lax.dot_general(left, right, (((1,), (1,)), ((), ())), preferred_element_type=f32)


def dot_nn(left, right):
    return lax.dot_general(left, right, (((1,), (0,)), ((), ())), preferred_element_type=f32)


def fold8(block):
    total = block[0:8]
    for k in range(8, block.shape[0], 8):
        total = total + block[k : k + 8]
    return total


def kernel(
    view1, view2, in1, in2, scale_ref,
    loss_ref, w1_ref, w2_ref,
    V1, V2, D1, D2, X1, X2, P1, P2, PT,
    zs, zr, cs, cr, xs, xr, ys, yr, U1, U2,
    C, G, GH, GL, M1, M2, A1, R1, A2, R2, AL, RL,
    ssem, rsem, lsem,
):
    R = view1.shape[0]
    B = V1.shape[0]
    T = V1.shape[1]
    dp = lax.axis_index("dp")
    ft = lax.axis_index("feat")
    c = lax.rem(dp, 2)
    x = lax.rem(lax.div(dp, 2), NX)
    yl = lax.div(dp, 2 * NX)
    yh = lax.rem(ft, 2)
    z = lax.div(ft, 2)

    def dpi(r, dx, other=0):
        y_ = yl if r == 0 else 1 - yl
        c_ = 1 - c if other else c
        return (y_ * NX + lax.rem(x + (dx % NX), NX)) * 2 + c_

    turn = 1 - 2 * c

    def fti(r, dz):
        y_ = yh if r == 0 else 1 - yh
        return lax.rem(z + NZ + dz * turn, NZ) * 2 + y_

    def rows(i):
        return pl.ds(pl.multiple_of(i * R, 16), R)

    def at(buf, i, u=None):
        if u is None:
            return buf.at[rows(i)]
        return buf.at[pl.ds(pl.multiple_of(i * R + PIECES[u][0], 16), PIECES[u][1])]

    def part(buf, slot, u):
        return buf.at[slot, pl.ds(*PIECES[u])]

    to_core = {"dp": dpi(0, 0, 1), "feat": ft}
    to_yl = {"dp": dpi(1, 0), "feat": ft}
    to_yh = {"dp": dp, "feat": fti(1, 0)}
    to = {
        "xp": {"dp": dpi(0, 1), "feat": ft},
        "xm": {"dp": dpi(0, -1), "feat": ft},
        "p": {"dp": dp, "feat": fti(0, 1)},
        "m": {"dp": dp, "feat": fti(0, -1)},
    }
    xa = x + 1 - 2 * lax.rem(x, 2)
    xb = NX - 1 - x
    za = z + 1 - 2 * lax.rem(z, 2)
    zb = z + 2 - 4 * lax.rem(lax.div(z, 2), 2)
    dp_steps = [
        to_core,
        to_yl,
        {"dp": (yl * NX + xa) * 2 + c, "feat": ft},
        {"dp": (yl * NX + xb) * 2 + c, "feat": ft},
    ]
    to_zb = {"dp": dp, "feat": zb * 2 + yh}
    to_zc = {"dp": dp, "feat": fti(0, 4)}
    feat_steps = [to_yh, {"dp": dp, "feat": za * 2 + yh}, to_zb, to_zc]

    peers = [to_core, to_yl, to_yh, to["xp"], to["xm"], to["p"], to["m"], to_zb, to_zc]
    barrier = pltpu.get_barrier_semaphore()
    for peer in peers:
        pl.semaphore_signal(barrier, inc=1, device_id=peer, device_id_type=MESH)
    local = [
        pltpu.make_async_copy(view1, at(V1, dp), lsem.at[0]),
        pltpu.make_async_copy(view2, at(V2, ft), lsem.at[1]),
        pltpu.make_async_copy(in1, X1, lsem.at[2]),
        pltpu.make_async_copy(in2, X2, lsem.at[3]),
    ]
    for copy in local:
        copy.start()
    pl.semaphore_wait(barrier, len(peers))

    names = {}

    def index(name):
        if name[0] in ("g", "d"):
            name = ("gather",) + name[1:]
        return names.setdefault(name, len(names))

    def group(name):
        if name[0] in ("g", "d"):
            return 0 if name[1] in ("yl", "xp", "xm", "c") else 1
        if name[0] == "s":
            return 2 if isinstance(name[1], tuple) else 3
        return ("a1", "a2", "al").index(name[0]) + 4

    def send(name, src, dst, dev):
        pltpu.make_async_remote_copy(
            src_ref=src, dst_ref=dst, send_sem=ssem.at[group(name)], recv_sem=rsem.at[index(name)],
            device_id=dev, device_id_type=MESH,
        ).start()

    def recv(name, dst):
        pltpu.make_async_remote_copy(
            src_ref=dst, dst_ref=dst, send_sem=ssem.at[0], recv_sem=rsem.at[index(name)],
            device_id=to_core, device_id_type=MESH,
        ).wait_recv()

    def drain(which, ref):
        pltpu.make_async_remote_copy(
            src_ref=ref, dst_ref=ref, send_sem=ssem.at[which], recv_sem=rsem.at[0],
            device_id=to_core, device_id_type=MESH,
        ).wait_send()

    def start_a(tag, A, src):
        own = at(A, dp)
        send((tag, "yl"), src, own, to_yl)
        send((tag, "xp", 0, 1), src, own, to["xp"])
        send((tag, "xm", 0, 1), src, own, to["xm"])
        send((tag, "c"), src, own, to_core)

    def start_b(tag, Bb, src, u):
        for d in ("p", "m"):
            send((tag, d, 0, 1, u), src.at[pl.ds(*PIECES[u])], at(Bb, ft, u), to[d])

    def ev_yl(tag, A):
        i = dpi(1, 0)
        recv((tag, "yl"), at(A, i))
        send((tag, "xp", 1, 1), at(A, i), at(A, i), to["xp"])
        send((tag, "xm", 1, 1), at(A, i), at(A, i), to["xm"])
        send((tag, "c"), at(A, i), at(A, i), to_core)
        return i

    def z_name(tag, d, r, h, u):
        return (tag, d, r, h) if (d, r, h) in FINAL else (tag, d, r, h, u)

    def ev_z(tag, Bb, d, r, h, u):
        i = fti(r, -h if d == "p" else h)
        if (d, r, h) in FINAL:
            if u == 0:
                recv((tag, d, r, h), at(Bb, i))
            return i
        piece = at(Bb, i, u)
        recv((tag, d, r, h, u), piece)
        if r == 0 and (d, h) in (("m", 1), ("p", 2)):
            send((tag, "y", d, h, u), piece, piece, to_yh)
        if h < (4 if d == "p" else 3):
            send(z_name(tag, d, r, h + 1, u), piece, piece, to[d])
        return i

    def ev_y(tag, Bb, d, h, u):
        i = fti(1, -h if d == "p" else h)
        piece = at(Bb, i, u)
        recv((tag, "y", d, h, u), piece)
        send(z_name(tag, d, 1, h + 1, u), piece, piece, to[d])
        return i

    def ev_x(tag, A, d, r, h):
        dx = (-SIGN[d] * h) % NX
        i = dpi(r, dx)
        recv((tag, d, r, h), at(A, i))
        if h < KX[d, r]:
            send((tag, d, r, h + 1), at(A, i), at(A, i), to[d])
        send((tag, "c"), at(A, i), at(A, i), to_core)
        return i

    def late_send(tag, Bb, n):
        block = at(Bb, fti(0, -n))
        send((tag, "y"), block, block, to_yh)

    def gather(tag, A, Bb, hook_a, hook_b, after):
        last = len(PIECES) - 1
        for n, steps in enumerate(ORDER):
            work = []
            for kind, *args in steps:
                if kind == "z" or kind == "y":
                    i = (ev_z if kind == "z" else ev_y)(tag, Bb, *args)
                    if n == len(ORDER) - 1:
                        hook_b(i, args[-1])
                    elif args[-1] == last:
                        work.append((hook_b, i))
                elif kind == "ls":
                    late_send(tag, Bb, *args)
                elif kind == "lr":
                    recv((tag, "y"), Bb.at[pl.ds(0, 2 * R)])
                    work += [(hook_b, fti(1, 0)), (hook_b, fti(1, -1))]
                elif kind == "yl":
                    work.append((hook_a, ev_yl(tag, A)))
                elif kind == "x":
                    work.append((hook_a, ev_x(tag, A, *args)))
                else:
                    recv((tag, "c"), A.at[pl.ds(0, len(CORDER) * R)])
                    work += [(hook_a, dpi(r, dx, 1)) for r, dx in CORDER]
            for hook, i in work:
                hook(i)
            if n in after:
                after[n]()

    CH = 48

    def span(u):
        return (0, R) if u is None else PIECES[u]

    def moments(V, M, i, u=None):
        start, count = span(u)
        base = i * R + start
        step = next(n for n in (48, 32, 16) if count % n == 0)

        def body(k, carry):
            s, q = carry
            v = V[pl.ds(pl.multiple_of(base + k * step, 16), step), :].astype(f32)
            return s + fold8(v), q + fold8(v * v)

        s, q = lax.fori_loop(0, count // step, body, (M[0:8, :], M[8:16, :]))
        M[0:8, :] = s
        M[8:16, :] = q

    def piece_rows(i, u):
        start, count = span(u)
        return pl.ds(pl.multiple_of(i * R + start, 16), count)

    def statistics(M):
        average = jnp.sum(M[0:8, :], axis=0, keepdims=True) / B
        spread = jnp.sum(M[8:16, :], axis=0, keepdims=True) / B - average * average
        M[16:24, :] = jnp.broadcast_to(lax.rsqrt(spread + epsilon), (8, T))
        M[32:40, :] = jnp.broadcast_to(average, (8, T))

    def normalize(V, M):
        average = M[32:33, :]
        inv = M[16:17, :]

        def body(k, total):
            at_ = pl.ds(pl.multiple_of(k * CH, 16), CH)
            n = ((V[at_, :].astype(f32) - average) * inv).astype(bf16)
            V[at_, :] = n
            return total + fold8(n.astype(f32))

        total = lax.fori_loop(0, B // CH, body, jnp.zeros((8, T), f32))
        M[24:32, :] = jnp.broadcast_to(jnp.sum(total, axis=0, keepdims=True), (8, T))

    M1[...] = jnp.zeros_like(M1)
    M2[...] = jnp.zeros_like(M2)
    for u in range(NP):
        start_b("g", V2, view2, u)
    start_a("g", V1, view1)
    local[0].wait()
    local[1].wait()
    moments(V1, M1, dp)
    moments(V2, M2, ft)

    ready = []
    waiting = [ft]

    def corr(i, u=None):
        at_ = piece_rows(i, u)
        C[...] += dot_tn(V1[at_, :], V2[at_, :])

    def work_two(i, u=None):
        moments(V2, M2, i, u)
        if ready:
            corr(i, u)
        else:
            waiting.append(i)

    def some(count):
        for _ in range(min(count, len(waiting))):
            corr(waiting.pop(0))

    def first_whole():
        drain(0, V1.at[pl.ds(0, 15 * R)])
        statistics(M1)
        normalize(V1, M1)
        C[...] = jnp.zeros_like(C)
        ready.append(True)
        some(4)

    after = {WHOLE: first_whole, WHOLE + 1: lambda: some(2), WHOLE + 2: lambda: some(4), WHOLE + 3: lambda: some(20)}
    gather("g", V1, V2, lambda i: moments(V1, M1, i), work_two, after)
    statistics(M2)

    KC = 768
    lane_row = lax.broadcasted_iota(jnp.int32, (16, T), 0)

    def split(value):
        high = value.astype(bf16).astype(f32)
        return high, value - high

    s_high, s_low = split(jnp.concatenate([M1[24:32, :], M1[24:32, :]], axis=0))
    a_high, a_low = split(jnp.concatenate([M2[32:40, :], M2[32:40, :]], axis=0))
    left = jnp.where(lane_row < 2, s_high, jnp.where(lane_row < 4, s_low, 0.0)).astype(bf16)
    right = jnp.where(lane_row % 2 == 0, a_high, a_low).astype(bf16)
    C[...] -= dot_tn(left, right)

    CG = 32
    scale = scale_ref[0]
    inv_two = M2[16:17, :] / B
    row0 = ft * T
    col0 = dp * T

    def grad(k, loss):
        at_ = pl.ds(pl.multiple_of(k * CG, CG), CG)
        corr_ = C[at_, :] * inv_two
        row_ids = row0 + k * CG + lax.broadcasted_iota(jnp.int32, (CG, T), 0)
        col_ids = col0 + lax.broadcasted_iota(jnp.int32, (CG, T), 1)
        on = row_ids == col_ids
        miss = 1.0 - corr_
        loss = loss + fold8(jnp.where(on, miss * miss, off_weight * corr_ * corr_))
        g = (jnp.where(on, -2.0 * miss, 2.0 * off_weight * corr_) * scale).astype(bf16)
        G[at_, :] = g
        prod = g.astype(f32) * corr_
        high = prod.astype(bf16)
        GH[at_, :] = high
        GL[at_, :] = (prod - high.astype(f32)).astype(bf16)
        return loss

    loss = lax.fori_loop(0, T // CG, grad, jnp.zeros((8, T), f32))
    loss_tile = loss[:, 0:128]
    for k in range(128, T, 128):
        loss_tile = loss_tile + loss[:, k : k + 128]

    DC = 16

    def delta(U, V, M, A, D, i, start, count):
        stats = A[4]
        first = stats[0:1, 0:T] / B
        second = stats[1:2, 0:T] / B
        inv = M[16:17, :]

        def body(k, carry):
            off = pl.multiple_of(start + k * DC, 16)
            at_ = pl.ds(pl.multiple_of(i * R + start + k * DC, 16), DC)
            own = V[at_, :].astype(f32)
            D[at_, :] = (inv * (U[pl.ds(off, DC), :] / B - first - own * second)).astype(bf16)
            return carry

        lax.fori_loop(0, count // DC, body, 0)

    def pair2(dz):
        at_ = pl.ds(pl.multiple_of(fti(0, dz) // 2 * (2 * R), 16), 2 * R)
        P2[at_, :] = dot_nn(V1[at_, :], G[...])

    def pair1(r, dx):
        PT[...] = dot_nt(V2[pl.ds(pl.multiple_of(dpi(r, dx) // 2 * (2 * R), 16), 2 * R), :], G[...])
        P1[CSLOT[r, dx]] = PT[rows(c), :]

    def p2(i, u):
        return P2[pl.ds(pl.multiple_of(i * R + PIECES[u][0], 16), PIECES[u][1]), :]

    def arrived(key, u):
        slot = ZSLOT[key]
        recv(("s", key, u), part(zr, slot, u))
        return part(zr, slot, u)[...].astype(f32)

    def zc(u, r, k, over_y=False, take=()):
        key = ("y", k) if over_y else (r, k)
        dev = to_yh if over_y else to["m"] if k > 0 else to["p"]
        val = p2(fti(r, -k), u)
        for source in take:
            val = val + arrived(source, u)
        part(zs, ZSLOT[key], u)[...] = val.astype(bf16)
        send(("s", key, u), part(zs, ZSLOT[key], u), part(zr, ZSLOT[key], u), dev)

    def z_end(u):
        val = p2(fti(0, 0), u)
        for source in ((0, 1), (0, -1), ("y", 0)):
            val = val + arrived(source, u)
        U2[pl.ds(*PIECES[u]), :] = val
        delta(U2, V2, M2, A2, D2, ft, *PIECES[u])
        start_b("d", D2, at(D2, ft), u)

    def far(u):
        if u == 0:
            pair2(-4)
            pair2(3)
        zc(u, 1, 4)
        zc(u, 1, -3)

    def far_own(u):
        zc(u, 0, 4)
        zc(u, 0, -3)

    def middle(u):
        if u == 0:
            pair2(-3)
            pair2(2)
        zc(u, 1, 3, take=[(1, 4)])
        zc(u, 1, -2, take=[(1, -3)])

    def middle_own(u):
        zc(u, 0, 3, take=[(0, 4)])
        zc(u, 0, -2, take=[(0, -3)])

    def cross(u):
        if u == 0:
            pair2(-2)
            pair2(1)
        zc(u, 1, 2, True, take=[(1, 3)])
        zc(u, 1, -1, True, take=[(1, -2)])

    def near(u):
        zc(u, 0, 2, take=[(0, 3), ("y", 2)])
        zc(u, 0, -1, take=[(0, -2), ("y", -1)])

    def nearest(u):
        zc(u, 0, 1, take=[(0, 2), ("y", 1)])

    def core_send(r, dx):
        pair1(r, dx)
        slot = CSLOT[r, dx]
        cs[slot] = PT[rows(1 - c), :].astype(bf16)
        send(("s", "c", slot >= 2), cs.at[slot], cr.at[slot], to_core)

    def both(r, dx):
        dx = dx % NX
        slot = CSLOT[r, dx]
        val = P1[slot]
        if slot == 0:
            recv(("s", "c", False), cr.at[pl.ds(0, 2)])
        if slot == 2:
            recv(("s", "c", True), cr.at[pl.ds(2, 6)])
        return val + cr[slot].astype(f32)

    def xc(d, r, s):
        val = both(r, SIGN[d] * (KX[d, r] - s))
        if s:
            prev = XSLOT[d, r, s - 1]
            recv(("s", d, r, s - 1), xr.at[prev])
            val = val + xr[prev].astype(f32)
        slot = XSLOT[d, r, s]
        xs[slot] = val.astype(bf16)
        send(("s", d, r, s), xs.at[slot], xr.at[slot], to[d])

    def x_end(r):
        val = both(r, 0)
        for d in ("xp", "xm"):
            last = KX[d, r] - 1
            slot = XSLOT[d, r, last]
            recv(("s", d, r, last), xr.at[slot])
            val = val + xr[slot].astype(f32)
        return val

    far(0)
    far(1)
    drain(1, V2.at[pl.ds(0, 15 * R)])
    normalize(V2, M2)
    pair2(-1)
    zc(0, 1, 1, True)
    zc(1, 1, 1, True)
    for r, dx in CORDER[0:4]:
        core_send(r, dx)
    middle(0)
    far_own(0)
    xc("xp", 0, 0)
    xc("xm", 1, 0)
    middle(1)
    for r, dx in CORDER[4:8]:
        core_send(r, dx)
    far_own(1)

    ones = jnp.ones((16, T), bf16)
    second1 = dot_nt(ones, GH[...]) + dot_nt(ones, GL[...])
    second2 = dot_nn(ones, GH[...]) + dot_nn(ones, GL[...])

    def split_rows(M):
        s = jnp.concatenate([M[24:32, :], M[24:32, :]], axis=0)
        high = s.astype(bf16).astype(f32)
        low = s - high
        return jnp.where(lane_row == 0, high, jnp.where(lane_row == 1, low, 0.0)).astype(bf16)

    first1 = jnp.sum(dot_nt(split_rows(M2), G[...]), axis=0, keepdims=True) / B
    first2 = jnp.sum(dot_nn(split_rows(M1), G[...]), axis=0, keepdims=True) / B
    top = lane_row[0:8] == 0
    A1[0, :, 0:T] = jnp.where(top, jnp.broadcast_to(first1, (8, T)), second1[0:8])
    A1[0, :, T : T + 128] = loss_tile
    A2[0] = jnp.where(top, jnp.broadcast_to(first2, (8, T)), second2[0:8])

    def put(n):
        send(("a1", n), A1.at[n], R1.at[n], dp_steps[n])
        send(("a2", n), A2.at[n], R2.at[n], feat_steps[n])

    def take(n):
        recv(("a1", n), R1.at[n])
        recv(("a2", n), R2.at[n])
        A1[n + 1] = A1[n] + R1[n]
        A2[n + 1] = A2[n] + R2[n]

    put(0)
    cross(0)
    xc("xp", 1, 0)
    xc("xm", 0, 0)
    middle_own(0)
    take(0)
    put(1)
    cross(1)
    middle_own(1)
    xc("xp", 0, 1)
    xc("xm", 1, 1)
    take(1)
    put(2)
    pair2(0)
    zc(0, 1, 0, True)
    zc(1, 1, 0, True)
    near(0)
    take(2)
    put(3)
    ys[0] = x_end(1).astype(bf16)
    send(("s", "yl"), ys.at[0], yr.at[0], to_yl)
    near(1)
    take(3)
    nearest(0)
    val = x_end(0)
    recv(("s", "yl"), yr.at[0])
    U1[...] = val + yr[0].astype(f32)
    delta(U1, V1, M1, A1, D1, dp, 0, R)
    start_a("d", D1, at(D1, dp))
    AL[0] = A1[4, :, T : T + 128]

    def put_l(n):
        send(("al", n), AL.at[n], RL.at[n], feat_steps[n])

    def take_l(n):
        recv(("al", n), RL.at[n])
        AL[n + 1] = AL[n] + RL[n]

    put_l(0)
    nearest(1)
    z_end(0)
    take_l(0)
    put_l(1)
    z_end(1)
    local[2].wait()
    local[3].wait()

    def weight(w_ref, X, D, i, u=None, first=False):
        at_ = piece_rows(i, u)
        term = dot_tn(X[at_, :], D[at_, :])
        if first:
            w_ref[...] = term
        else:
            w_ref[...] += term

    def weights_one():
        w1_ref[...] = dot_tn(X1[0:KC, :], D1[0:KC, :])

        def body(k, carry):
            at_ = pl.ds(pl.multiple_of(k * KC, 16), KC)
            w1_ref[...] += dot_tn(X1[at_, :], D1[at_, :])
            return carry

        lax.fori_loop(1, B // KC, body, 0)

    def loss_step(n):
        take_l(n)
        if n < 3:
            put_l(n + 1)
        else:
            loss_ref[0] = jnp.sum(AL[4]) / F

    weight(w2_ref, X2, D2, ft, first=True)
    after = {0: lambda: loss_step(1), 2: lambda: loss_step(2), 4: lambda: loss_step(3), WHOLE: weights_one}
    gather("d", D1, D2, lambda i: None, lambda i, u=None: weight(w2_ref, X2, D2, i, u), after)
    drain(0, D1.at[pl.ds(0, 15 * R)])
    drain(1, D2.at[pl.ds(0, 15 * R)])
    drain(2, zs)
    drain(3, zs)
    drain(4, A1.at[pl.ds(0, 4)])
    drain(5, A2.at[pl.ds(0, 4)])
    drain(6, AL.at[pl.ds(0, 4)])
    assert len(names) == NSEM, len(names)


def per_device(view_one, view_two, inputs_one, inputs_two, loss_scale):
    R, T = view_one.shape
    B = inputs_one.shape[0]
    block = (R, T)
    anywhere = pl.BlockSpec(memory_space=pl.ANY)
    vmem = pl.BlockSpec(memory_space=pltpu.VMEM)
    smem = pl.BlockSpec(memory_space=pltpu.SMEM)
    V = pltpu.VMEM
    scratch = [
        V((B, T), bf16), V((B, T), bf16), V((B, T), bf16), V((B, T), bf16),
        V((B, T), bf16), V((B, T), bf16), V((len(CSLOT),) + block, f32), V((B, T), f32), V((2 * R, T), f32),
        V((len(ZSLOT),) + block, bf16), V((len(ZSLOT),) + block, bf16),
        V((len(CSLOT),) + block, bf16), V((len(CSLOT),) + block, bf16),
        V((len(XSLOT),) + block, bf16), V((len(XSLOT),) + block, bf16),
        V((1,) + block, bf16), V((1,) + block, bf16),
        V(block, f32), V(block, f32),
        V((T, T), f32), V((T, T), bf16), V((T, T), bf16), V((T, T), bf16),
        V((40, T), f32), V((40, T), f32),
        V((5, 8, T + 128), f32), V((4, 8, T + 128), f32),
        V((5, 8, T), f32), V((4, 8, T), f32),
        V((5, 8, 128), f32), V((4, 8, 128), f32),
        pltpu.SemaphoreType.DMA((7,)),
        pltpu.SemaphoreType.DMA((NSEM,)),
        pltpu.SemaphoreType.DMA((4,)),
    ]
    return pl.pallas_call(
        kernel,
        out_shape=(
            jax.ShapeDtypeStruct((1,), f32),
            V((T, T), f32),
            V((T, T), f32),
        ),
        in_specs=[anywhere] * 4 + [smem],
        out_specs=(smem, vmem, vmem),
        scratch_shapes=scratch,
        compiler_params=pltpu.CompilerParams(
            collective_id=0, has_side_effects=True, vmem_limit_bytes=59 * 1024 * 1024
        ),
        cost_estimate=pl.CostEstimate(
            flops=10 * B * T * T, bytes_accessed=4 * B * T + 8 * T * T, transcendentals=0
        ),
    )(view_one, view_two, inputs_one, inputs_two, loss_scale)


def solution(mesh):
    placed = (P("dp", "feat"), P("feat", "dp"), P(None, "dp"), P(None, "feat"), P())
    return jax.shard_map(
        per_device,
        mesh=mesh,
        in_specs=placed,
        out_specs=(P(), P("dp", "feat"), P("feat", "dp")),
        check_vma=False,
    )
```

```python
import jax
import jax.numpy as jnp
from jax import lax
from jax.experimental import pallas as pl
from jax.experimental.pallas import tpu as pltpu
from jax.sharding import PartitionSpec as P

F = 8192
off_weight = 0.0051
epsilon = 1e-05
MESH = pl.DeviceIdType.MESH
f32 = jnp.float32
bf16 = jnp.bfloat16

NX = 4
NZ = 8
SIGN = {"xp": 1, "xm": -1}
KX = {("xp", 0): 2, ("xm", 0): 1, ("xp", 1): 1, ("xm", 1): 2}
PIECES = ((0, 128), (128, 112))
NP = len(PIECES)
ZSLOT = {
    key: n
    for n, key in enumerate(
        [(1, 4), (1, 3), (1, -3), (1, -2), (0, 4), (0, 3), (0, 2), (0, 1), (0, -3), (0, -2), (0, -1)]
        + [("y", 2), ("y", -1), ("y", 1), ("y", 0)]
    )
}
XSLOT = {}
for key, hops in KX.items():
    for hop in range(hops):
        XSLOT[key + (hop,)] = len(XSLOT)
CORDER = [(0, 2), (1, 2), (1, 1), (0, 3), (0, 1), (1, 3), (1, 0), (0, 0)]
CSLOT = {key: n for n, key in enumerate(CORDER)}
NSEM = 83
FINAL = (("p", 0, 4), ("m", 0, 3), ("m", 1, 3))

def both_z(r, hp, hm):
    return [("z", d, r, h, u) for u in range(NP) for d, h in (("p", hp), ("m", hm)) if h]


def one_z(d, r, h):
    return [("z", d, r, h, u) for u in range(NP)]


def over_y(d, h):
    return [("y", d, h, u) for u in range(NP)]


ORDER = [
    both_z(0, 1, 1),
    [("yl",), ("x", "xp", 0, 1), ("x", "xm", 0, 1)],
    both_z(0, 2, 2),
    [("x", "xp", 1, 1), ("x", "xm", 1, 1)] + over_y("m", 1) + [("ls", 0)],
    both_z(0, 3, 3),
    [("x", "xp", 0, 2), ("x", "xm", 1, 2)] + over_y("p", 2) + [("ls", 1)],
    one_z("m", 1, 2),
    [("c",)],
    one_z("p", 1, 3),
    one_z("p", 0, 4),
    one_z("m", 1, 3),
    [("lr",)],
    one_z("p", 1, 4),
]
WHOLE = 7


def dot_tn(left, right):
    return lax.dot_general(left, right, (((0,), (0,)), ((), ())), preferred_element_type=f32)


def dot_nt(left, right):
    return lax.dot_general(left, right, (((1,), (1,)), ((), ())), preferred_element_type=f32)


def dot_nn(left, right):
    return lax.dot_general(left, right, (((1,), (0,)), ((), ())), preferred_element_type=f32)


def fold8(block):
    total = block[0:8]
    for k in range(8, block.shape[0], 8):
        total = total + block[k : k + 8]
    return total


def kernel(
    view1, view2, in1, in2, scale_ref,
    loss_ref, w1_ref, w2_ref,
    V1, V2, D1, D2, X1, X2, P1, P2, PT,
    zs, zr, cs, cr, xs, xr, ys, yr, U1, U2,
    C, G, GH, GL, M1, M2, A1, R1, A2, R2, AL, RL,
    ssem, rsem, lsem,
):
    R = view1.shape[0]
    B = V1.shape[0]
    T = V1.shape[1]
    dp = lax.axis_index("dp")
    ft = lax.axis_index("feat")
    c = lax.rem(dp, 2)
    x = lax.rem(lax.div(dp, 2), NX)
    yl = lax.div(dp, 2 * NX)
    yh = lax.rem(ft, 2)
    z = lax.div(ft, 2)

    def dpi(r, dx, other=0):
        y_ = yl if r == 0 else 1 - yl
        c_ = 1 - c if other else c
        return (y_ * NX + lax.rem(x + (dx % NX), NX)) * 2 + c_

    turn = 1 - 2 * c

    def fti(r, dz):
        y_ = yh if r == 0 else 1 - yh
        return lax.rem(z + NZ + dz * turn, NZ) * 2 + y_

    def rows(i):
        return pl.ds(pl.multiple_of(i * R, 16), R)

    def at(buf, i, u=None):
        if u is None:
            return buf.at[rows(i)]
        return buf.at[pl.ds(pl.multiple_of(i * R + PIECES[u][0], 16), PIECES[u][1])]

    def part(buf, slot, u):
        return buf.at[slot, pl.ds(*PIECES[u])]

    to_core = {"dp": dpi(0, 0, 1), "feat": ft}
    to_yl = {"dp": dpi(1, 0), "feat": ft}
    to_yh = {"dp": dp, "feat": fti(1, 0)}
    to = {
        "xp": {"dp": dpi(0, 1), "feat": ft},
        "xm": {"dp": dpi(0, -1), "feat": ft},
        "p": {"dp": dp, "feat": fti(0, 1)},
        "m": {"dp": dp, "feat": fti(0, -1)},
    }
    xa = x + 1 - 2 * lax.rem(x, 2)
    xb = NX - 1 - x
    za = z + 1 - 2 * lax.rem(z, 2)
    zb = z + 2 - 4 * lax.rem(lax.div(z, 2), 2)
    dp_steps = [
        to_core,
        to_yl,
        {"dp": (yl * NX + xa) * 2 + c, "feat": ft},
        {"dp": (yl * NX + xb) * 2 + c, "feat": ft},
    ]
    to_zb = {"dp": dp, "feat": zb * 2 + yh}
    to_zc = {"dp": dp, "feat": fti(0, 4)}
    feat_steps = [to_yh, {"dp": dp, "feat": za * 2 + yh}, to_zb, to_zc]

    peers = [to_core, to_yl, to_yh, to["xp"], to["xm"], to["p"], to["m"], to_zb, to_zc]
    barrier = pltpu.get_barrier_semaphore()
    for peer in peers:
        pl.semaphore_signal(barrier, inc=1, device_id=peer, device_id_type=MESH)
    local = [
        pltpu.make_async_copy(view1, at(V1, dp), lsem.at[0]),
        pltpu.make_async_copy(view2, at(V2, ft), lsem.at[1]),
        pltpu.make_async_copy(in1, X1, lsem.at[2]),
        pltpu.make_async_copy(in2, X2, lsem.at[3]),
    ]
    for copy in local:
        copy.start()
    pl.semaphore_wait(barrier, len(peers))

    names = {}

    def index(name):
        if name[0] in ("g", "d"):
            name = ("gather",) + name[1:]
        return names.setdefault(name, len(names))

    def group(name):
        if name[0] in ("g", "d"):
            return 0 if name[1] in ("yl", "xp", "xm", "c") else 1
        if name[0] == "s":
            return 2 if isinstance(name[1], tuple) else 3
        return ("a1", "a2", "al").index(name[0]) + 4

    def send(name, src, dst, dev):
        pltpu.make_async_remote_copy(
            src_ref=src, dst_ref=dst, send_sem=ssem.at[group(name)], recv_sem=rsem.at[index(name)],
            device_id=dev, device_id_type=MESH,
        ).start()

    def recv(name, dst):
        pltpu.make_async_remote_copy(
            src_ref=dst, dst_ref=dst, send_sem=ssem.at[0], recv_sem=rsem.at[index(name)],
            device_id=to_core, device_id_type=MESH,
        ).wait_recv()

    def drain(which, ref):
        pltpu.make_async_remote_copy(
            src_ref=ref, dst_ref=ref, send_sem=ssem.at[which], recv_sem=rsem.at[0],
            device_id=to_core, device_id_type=MESH,
        ).wait_send()

    def start_a(tag, A, src):
        own = at(A, dp)
        send((tag, "yl"), src, own, to_yl)
        send((tag, "xp", 0, 1), src, own, to["xp"])
        send((tag, "xm", 0, 1), src, own, to["xm"])
        send((tag, "c"), src, own, to_core)

    def start_b(tag, Bb, src, u):
        for d in ("p", "m"):
            send((tag, d, 0, 1, u), src.at[pl.ds(*PIECES[u])], at(Bb, ft, u), to[d])

    def ev_yl(tag, A):
        i = dpi(1, 0)
        recv((tag, "yl"), at(A, i))
        send((tag, "xp", 1, 1), at(A, i), at(A, i), to["xp"])
        send((tag, "xm", 1, 1), at(A, i), at(A, i), to["xm"])
        send((tag, "c"), at(A, i), at(A, i), to_core)
        return i

    def z_name(tag, d, r, h, u):
        return (tag, d, r, h) if (d, r, h) in FINAL else (tag, d, r, h, u)

    def ev_z(tag, Bb, d, r, h, u):
        i = fti(r, -h if d == "p" else h)
        if (d, r, h) in FINAL:
            if u == 0:
                recv((tag, d, r, h), at(Bb, i))
            return i
        piece = at(Bb, i, u)
        recv((tag, d, r, h, u), piece)
        if r == 0 and (d, h) in (("m", 1), ("p", 2)):
            send((tag, "y", d, h, u), piece, piece, to_yh)
        if h < (4 if d == "p" else 3):
            send(z_name(tag, d, r, h + 1, u), piece, piece, to[d])
        return i

    def ev_y(tag, Bb, d, h, u):
        i = fti(1, -h if d == "p" else h)
        piece = at(Bb, i, u)
        recv((tag, "y", d, h, u), piece)
        send(z_name(tag, d, 1, h + 1, u), piece, piece, to[d])
        return i

    def ev_x(tag, A, d, r, h):
        dx = (-SIGN[d] * h) % NX
        i = dpi(r, dx)
        recv((tag, d, r, h), at(A, i))
        if h < KX[d, r]:
            send((tag, d, r, h + 1), at(A, i), at(A, i), to[d])
        send((tag, "c"), at(A, i), at(A, i), to_core)
        return i

    def late_send(tag, Bb, n):
        block = at(Bb, fti(0, -n))
        send((tag, "y"), block, block, to_yh)

    def gather(tag, A, Bb, hook_a, hook_b, after):
        last = len(PIECES) - 1
        for n, steps in enumerate(ORDER):
            work = []
            for kind, *args in steps:
                if kind == "z" or kind == "y":
                    i = (ev_z if kind == "z" else ev_y)(tag, Bb, *args)
                    if n == len(ORDER) - 1:
                        hook_b(i, args[-1])
                    elif args[-1] == last:
                        work.append((hook_b, i))
                elif kind == "ls":
                    late_send(tag, Bb, *args)
                elif kind == "lr":
                    recv((tag, "y"), Bb.at[pl.ds(0, 2 * R)])
                    work += [(hook_b, fti(1, 0)), (hook_b, fti(1, -1))]
                elif kind == "yl":
                    work.append((hook_a, ev_yl(tag, A)))
                elif kind == "x":
                    work.append((hook_a, ev_x(tag, A, *args)))
                else:
                    recv((tag, "c"), A.at[pl.ds(0, len(CORDER) * R)])
                    work += [(hook_a, dpi(r, dx, 1)) for r, dx in CORDER]
            for hook, i in work:
                hook(i)
            if n in after:
                after[n]()

    CH = 48

    def span(u):
        return (0, R) if u is None else PIECES[u]

    def moments(V, M, i, u=None):
        start, count = span(u)
        base = i * R + start
        step = next(n for n in (48, 32, 16) if count % n == 0)

        def body(k, carry):
            s, q = carry
            v = V[pl.ds(pl.multiple_of(base + k * step, 16), step), :].astype(f32)
            return s + fold8(v), q + fold8(v * v)

        s, q = lax.fori_loop(0, count // step, body, (M[0:8, :], M[8:16, :]))
        M[0:8, :] = s
        M[8:16, :] = q

    def piece_rows(i, u):
        start, count = span(u)
        return pl.ds(pl.multiple_of(i * R + start, 16), count)

    def statistics(M):
        average = jnp.sum(M[0:8, :], axis=0, keepdims=True) / B
        spread = jnp.sum(M[8:16, :], axis=0, keepdims=True) / B - average * average
        M[16:24, :] = jnp.broadcast_to(lax.rsqrt(spread + epsilon), (8, T))
        M[32:40, :] = jnp.broadcast_to(average, (8, T))

    def normalize(V, M):
        average = M[32:33, :]
        inv = M[16:17, :]

        def body(k, total):
            at_ = pl.ds(pl.multiple_of(k * CH, 16), CH)
            n = ((V[at_, :].astype(f32) - average) * inv).astype(bf16)
            V[at_, :] = n
            return total + fold8(n.astype(f32))

        total = lax.fori_loop(0, B // CH, body, jnp.zeros((8, T), f32))
        M[24:32, :] = jnp.broadcast_to(jnp.sum(total, axis=0, keepdims=True), (8, T))

    M1[...] = jnp.zeros_like(M1)
    M2[...] = jnp.zeros_like(M2)
    for u in range(NP):
        start_b("g", V2, view2, u)
    start_a("g", V1, view1)
    local[0].wait()
    local[1].wait()
    moments(V1, M1, dp)
    moments(V2, M2, ft)

    ready = []
    waiting = [ft]

    def corr(i, u=None):
        at_ = piece_rows(i, u)
        C[...] += dot_tn(V1[at_, :], V2[at_, :])

    def work_two(i, u=None):
        moments(V2, M2, i, u)
        if ready:
            corr(i, u)
        else:
            waiting.append(i)

    def some(count):
        for _ in range(min(count, len(waiting))):
            corr(waiting.pop(0))

    def first_whole():
        drain(0, V1.at[pl.ds(0, 15 * R)])
        statistics(M1)
        normalize(V1, M1)
        C[...] = jnp.zeros_like(C)
        ready.append(True)
        some(3)

    after = {WHOLE: first_whole, WHOLE + 1: lambda: some(3), WHOLE + 2: lambda: some(5), WHOLE + 3: lambda: some(20)}
    gather("g", V1, V2, lambda i: moments(V1, M1, i), work_two, after)
    statistics(M2)

    KC = 768
    lane_row = lax.broadcasted_iota(jnp.int32, (16, T), 0)

    def split(value):
        high = value.astype(bf16).astype(f32)
        return high, value - high

    s_high, s_low = split(jnp.concatenate([M1[24:32, :], M1[24:32, :]], axis=0))
    a_high, a_low = split(jnp.concatenate([M2[32:40, :], M2[32:40, :]], axis=0))
    left = jnp.where(lane_row < 2, s_high, jnp.where(lane_row < 4, s_low, 0.0)).astype(bf16)
    right = jnp.where(lane_row % 2 == 0, a_high, a_low).astype(bf16)
    C[...] -= dot_tn(left, right)

    CG = 32
    scale = scale_ref[0]
    inv_two = M2[16:17, :] / B
    row0 = ft * T
    col0 = dp * T

    def tile(k):
        at_ = pl.ds(pl.multiple_of(k * CG, CG), CG)
        corr_ = C[at_, :] * inv_two
        row_ids = row0 + k * CG + lax.broadcasted_iota(jnp.int32, (CG, T), 0)
        col_ids = col0 + lax.broadcasted_iota(jnp.int32, (CG, T), 1)
        return at_, corr_, row_ids == col_ids, 1.0 - corr_

    def grad(k, carry):
        at_, corr_, on, miss = tile(k)
        G[at_, :] = (jnp.where(on, -2.0 * miss, 2.0 * off_weight * corr_) * scale).astype(bf16)
        return carry

    lax.fori_loop(0, T // CG, grad, 0)

    def terms(k, loss):
        at_, corr_, on, miss = tile(k)
        prod = G[at_, :].astype(f32) * corr_
        high = prod.astype(bf16)
        GH[at_, :] = high
        GL[at_, :] = (prod - high.astype(f32)).astype(bf16)
        return loss + fold8(jnp.where(on, miss * miss, off_weight * corr_ * corr_))

    DC = 16

    def delta(U, V, M, A, D, i, start, count):
        stats = A[4]
        first = jnp.concatenate([stats[k : k + 1] for k in range(4)], axis=1) / B
        second = jnp.concatenate([stats[k : k + 1] for k in range(4, 8)], axis=1) / B
        inv = M[16:17, :]

        def body(k, carry):
            off = pl.multiple_of(start + k * DC, 16)
            at_ = pl.ds(pl.multiple_of(i * R + start + k * DC, 16), DC)
            own = V[at_, :].astype(f32)
            D[at_, :] = (inv * (U[pl.ds(off, DC), :] / B - first - own * second)).astype(bf16)
            return carry

        lax.fori_loop(0, count // DC, body, 0)

    def pair2(dz):
        at_ = pl.ds(pl.multiple_of(fti(0, dz) // 2 * (2 * R), 16), 2 * R)
        P2[at_, :] = dot_nn(V1[at_, :], G[...])

    def pair1(r, dx):
        PT[...] = dot_nt(V2[pl.ds(pl.multiple_of(dpi(r, dx) // 2 * (2 * R), 16), 2 * R), :], G[...])
        P1[CSLOT[r, dx]] = PT[rows(c), :]

    def p2(i, u):
        return P2[pl.ds(pl.multiple_of(i * R + PIECES[u][0], 16), PIECES[u][1]), :]

    def arrived(key, u):
        slot = ZSLOT[key]
        recv(("s", key, u), part(zr, slot, u))
        return part(zr, slot, u)[...].astype(f32)

    def zc(u, r, k, over_y=False, take=()):
        key = ("y", k) if over_y else (r, k)
        dev = to_yh if over_y else to["m"] if k > 0 else to["p"]
        val = p2(fti(r, -k), u)
        for source in take:
            val = val + arrived(source, u)
        part(zs, ZSLOT[key], u)[...] = val.astype(bf16)
        send(("s", key, u), part(zs, ZSLOT[key], u), part(zr, ZSLOT[key], u), dev)

    def z_end(u):
        val = p2(fti(0, 0), u)
        for source in ((0, 1), (0, -1), ("y", 0)):
            val = val + arrived(source, u)
        U2[pl.ds(*PIECES[u]), :] = val
        delta(U2, V2, M2, A2, D2, ft, *PIECES[u])
        start_b("d", D2, at(D2, ft), u)

    def far(u):
        if u == 0:
            pair2(-4)
        zc(u, 1, 4)
        if u == 0:
            pair2(3)
        zc(u, 1, -3)

    def far_own(u):
        zc(u, 0, 4)
        zc(u, 0, -3)

    def middle(u):
        if u == 0:
            pair2(-3)
            pair2(2)
        zc(u, 1, 3, take=[(1, 4)])
        zc(u, 1, -2, take=[(1, -3)])

    def middle_own(u):
        zc(u, 0, 3, take=[(0, 4)])
        zc(u, 0, -2, take=[(0, -3)])

    def cross(u):
        if u == 0:
            pair2(-2)
            pair2(1)
        zc(u, 1, 2, True, take=[(1, 3)])
        zc(u, 1, -1, True, take=[(1, -2)])

    def near(u):
        zc(u, 0, 2, take=[(0, 3), ("y", 2)])
        zc(u, 0, -1, take=[(0, -2), ("y", -1)])

    def nearest(u):
        zc(u, 0, 1, take=[(0, 2), ("y", 1)])

    def core_send(r, dx):
        pair1(r, dx)
        slot = CSLOT[r, dx]
        cs[slot] = PT[rows(1 - c), :].astype(bf16)
        send(("s", "c", slot >= 2), cs.at[slot], cr.at[slot], to_core)

    def both(r, dx):
        dx = dx % NX
        slot = CSLOT[r, dx]
        val = P1[slot]
        if slot == 0:
            recv(("s", "c", False), cr.at[pl.ds(0, 2)])
        if slot == 2:
            recv(("s", "c", True), cr.at[pl.ds(2, 6)])
        return val + cr[slot].astype(f32)

    def xc(d, r, s):
        val = both(r, SIGN[d] * (KX[d, r] - s))
        if s:
            prev = XSLOT[d, r, s - 1]
            recv(("s", d, r, s - 1), xr.at[prev])
            val = val + xr[prev].astype(f32)
        slot = XSLOT[d, r, s]
        xs[slot] = val.astype(bf16)
        send(("s", d, r, s), xs.at[slot], xr.at[slot], to[d])

    def x_end(r):
        val = both(r, 0)
        for d in ("xp", "xm"):
            last = KX[d, r] - 1
            slot = XSLOT[d, r, last]
            recv(("s", d, r, last), xr.at[slot])
            val = val + xr[slot].astype(f32)
        return val

    far(0)
    far(1)
    drain(1, V2.at[pl.ds(0, 15 * R)])
    normalize(V2, M2)
    pair2(-1)
    zc(0, 1, 1, True)
    zc(1, 1, 1, True)
    for r, dx in CORDER[0:4]:
        core_send(r, dx)
    middle(0)
    far_own(0)
    xc("xp", 0, 0)
    xc("xm", 1, 0)
    middle(1)
    for r, dx in CORDER[4:8]:
        core_send(r, dx)
    far_own(1)
    cross(0)
    xc("xp", 1, 0)
    xc("xm", 0, 0)
    cross(1)
    middle_own(0)
    def put(n):
        send(("a1", n), A1.at[n], R1.at[n], dp_steps[n])
        send(("a2", n), A2.at[n], R2.at[n], feat_steps[n])

    def take(n):
        recv(("a1", n), R1.at[n])
        recv(("a2", n), R2.at[n])
        A1[n + 1] = A1[n] + R1[n]
        A2[n + 1] = A2[n] + R2[n]

    loss = lax.fori_loop(0, T // CG, terms, jnp.zeros((8, T), f32))
    loss_tile = loss[:, 0:128]
    for k in range(128, T, 128):
        loss_tile = loss_tile + loss[:, k : k + 128]

    ones = jnp.ones((16, T), bf16)
    second1 = dot_nt(ones, GH[...]) + dot_nt(ones, GL[...])
    second2 = dot_nn(ones, GH[...]) + dot_nn(ones, GL[...])

    def split_rows(M):
        s = jnp.concatenate([M[24:32, :], M[24:32, :]], axis=0)
        high = s.astype(bf16).astype(f32)
        low = s - high
        return jnp.where(lane_row == 0, high, jnp.where(lane_row == 1, low, 0.0)).astype(bf16)

    first1 = jnp.sum(dot_nt(split_rows(M2), G[...]), axis=0, keepdims=True) / B
    first2 = jnp.sum(dot_nn(split_rows(M1), G[...]), axis=0, keepdims=True) / B

    for k in range(T // 128):
        lanes = slice(k * 128, k * 128 + 128)
        A1[0, k : k + 1, :] = first1[:, lanes]
        A1[0, 4 + k : 5 + k, :] = second1[0:1, lanes]
        A2[0, k : k + 1, :] = first2[:, lanes]
        A2[0, 4 + k : 5 + k, :] = second2[0:1, lanes]
    A1[0, 8:16, :] = loss_tile

    put(0)
    middle_own(1)
    xc("xp", 0, 1)
    xc("xm", 1, 1)
    pair2(0)
    zc(0, 1, 0, True)
    zc(1, 1, 0, True)
    take(0)
    put(1)
    near(0)
    near(1)
    take(1)
    put(2)
    ys[0] = x_end(1).astype(bf16)
    send(("s", "yl"), ys.at[0], yr.at[0], to_yl)
    take(2)
    put(3)

    nearest(0)
    take(3)
    nearest(1)
    z_end(0)
    val = x_end(0)
    recv(("s", "yl"), yr.at[0])
    U1[...] = val + yr[0].astype(f32)
    delta(U1, V1, M1, A1, D1, dp, 0, R)
    start_a("d", D1, at(D1, dp))
    z_end(1)
    AL[0] = A1[4, 8:16, :]

    def put_l(n):
        send(("al", n), AL.at[n], RL.at[n], feat_steps[n])

    def take_l(n):
        recv(("al", n), RL.at[n])
        AL[n + 1] = AL[n] + RL[n]

    put_l(0)
    take_l(0)
    put_l(1)

    local[2].wait()
    local[3].wait()

    def weight(w_ref, X, D, i, u=None, first=False):
        at_ = piece_rows(i, u)
        term = dot_tn(X[at_, :], D[at_, :])
        if first:
            w_ref[...] = term
        else:
            w_ref[...] += term

    def weights_one():
        w1_ref[...] = dot_tn(X1[0:KC, :], D1[0:KC, :])

        def body(k, carry):
            at_ = pl.ds(pl.multiple_of(k * KC, 16), KC)
            w1_ref[...] += dot_tn(X1[at_, :], D1[at_, :])
            return carry

        lax.fori_loop(1, B // KC, body, 0)

    def loss_step(n):
        take_l(n)
        if n < 3:
            put_l(n + 1)
        else:
            loss_ref[0] = jnp.sum(AL[4]) / F

    weight(w2_ref, X2, D2, ft, first=True)
    after = {0: lambda: loss_step(1), 2: lambda: loss_step(2), 4: lambda: loss_step(3), WHOLE: weights_one}
    gather("d", D1, D2, lambda i: None, lambda i, u=None: weight(w2_ref, X2, D2, i, u), after)
    drain(0, D1.at[pl.ds(0, 15 * R)])
    drain(1, D2.at[pl.ds(0, 15 * R)])
    drain(2, zs)
    drain(3, zs)
    drain(4, A1.at[pl.ds(0, 4)])
    drain(5, A2.at[pl.ds(0, 4)])
    drain(6, AL.at[pl.ds(0, 4)])
    assert len(names) == NSEM, len(names)


def per_device(view_one, view_two, inputs_one, inputs_two, loss_scale):
    R, T = view_one.shape
    B = inputs_one.shape[0]
    block = (R, T)
    anywhere = pl.BlockSpec(memory_space=pl.ANY)
    vmem = pl.BlockSpec(memory_space=pltpu.VMEM)
    smem = pl.BlockSpec(memory_space=pltpu.SMEM)
    V = pltpu.VMEM
    scratch = [
        V((B, T), bf16), V((B, T), bf16), V((B, T), bf16), V((B, T), bf16),
        V((B, T), bf16), V((B, T), bf16), V((len(CSLOT),) + block, f32), V((B, T), f32), V((2 * R, T), f32),
        V((len(ZSLOT),) + block, bf16), V((len(ZSLOT),) + block, bf16),
        V((len(CSLOT),) + block, bf16), V((len(CSLOT),) + block, bf16),
        V((len(XSLOT),) + block, bf16), V((len(XSLOT),) + block, bf16),
        V((1,) + block, bf16), V((1,) + block, bf16),
        V(block, f32), V(block, f32),
        V((T, T), f32), V((T, T), bf16), V((T, T), bf16), V((T, T), bf16),
        V((40, T), f32), V((40, T), f32),
        V((5, 16, 128), f32), V((4, 16, 128), f32),
        V((5, 8, 128), f32), V((4, 8, 128), f32),
        V((5, 8, 128), f32), V((4, 8, 128), f32),
        pltpu.SemaphoreType.DMA((7,)),
        pltpu.SemaphoreType.DMA((NSEM,)),
        pltpu.SemaphoreType.DMA((4,)),
    ]
    return pl.pallas_call(
        kernel,
        out_shape=(
            jax.ShapeDtypeStruct((1,), f32),
            V((T, T), f32),
            V((T, T), f32),
        ),
        in_specs=[anywhere] * 4 + [smem],
        out_specs=(smem, vmem, vmem),
        scratch_shapes=scratch,
        compiler_params=pltpu.CompilerParams(
            collective_id=0, has_side_effects=True, vmem_limit_bytes=59 * 1024 * 1024
        ),
        cost_estimate=pl.CostEstimate(
            flops=10 * B * T * T, bytes_accessed=4 * B * T + 8 * T * T, transcendentals=0
        ),
    )(view_one, view_two, inputs_one, inputs_two, loss_scale)


def solution(mesh):
    placed = (P("dp", "feat"), P("feat", "dp"), P(None, "dp"), P(None, "feat"), P())
    return jax.shard_map(
        per_device,
        mesh=mesh,
        in_specs=placed,
        out_specs=(P(), P("dp", "feat"), P("feat", "dp")),
        check_vma=False,
    )
```

```python
import jax
import jax.numpy as jnp
from jax import lax
from jax.experimental import pallas as pl
from jax.experimental.pallas import tpu as pltpu
from jax.sharding import PartitionSpec as P

F = 8192
off_weight = 0.0051
epsilon = 1e-05
MESH = pl.DeviceIdType.MESH
f32 = jnp.float32
bf16 = jnp.bfloat16

NX = 4
NZ = 8
SIGN = {"xp": 1, "xm": -1}
KX = {("xp", 0): 2, ("xm", 0): 1, ("xp", 1): 1, ("xm", 1): 2}
PIECES = ((0, 128), (128, 112))
NP = len(PIECES)
ZSLOT = {
    key: n
    for n, key in enumerate(
        [(1, 4), (1, 3), (1, -3), (1, -2), (0, 4), (0, 3), (0, 2), (0, 1), (0, -3), (0, -2), (0, -1)]
        + [("y", 2), ("y", -1), ("y", 1), ("y", 0)]
    )
}
XSLOT = {}
for key, hops in KX.items():
    for hop in range(hops):
        XSLOT[key + (hop,)] = len(XSLOT)
CORDER = [(0, 2), (1, 2), (1, 1), (0, 3), (0, 1), (1, 3), (1, 0), (0, 0)]
CSLOT = {key: n for n, key in enumerate(CORDER)}
NSEM = 83
FINAL = (("p", 0, 4), ("m", 0, 3), ("m", 1, 3))

def both_z(r, hp, hm):
    return [("z", d, r, h, u) for u in range(NP) for d, h in (("p", hp), ("m", hm)) if h]


def one_z(d, r, h):
    return [("z", d, r, h, u) for u in range(NP)]


def over_y(d, h):
    return [("y", d, h, u) for u in range(NP)]


ORDER = [
    both_z(0, 1, 1),
    [("yl",), ("x", "xp", 0, 1), ("x", "xm", 0, 1)],
    both_z(0, 2, 2),
    [("x", "xp", 1, 1), ("x", "xm", 1, 1)] + over_y("m", 1) + [("ls", 0)],
    both_z(0, 3, 3),
    [("x", "xp", 0, 2), ("x", "xm", 1, 2)] + over_y("p", 2) + [("ls", 1)],
    one_z("m", 1, 2),
    [("c",)],
    one_z("p", 1, 3),
    one_z("p", 0, 4),
    one_z("m", 1, 3),
    [("lr",)],
    one_z("p", 1, 4),
]
WHOLE = 7


def dot_tn(left, right):
    return lax.dot_general(left, right, (((0,), (0,)), ((), ())), preferred_element_type=f32)


def dot_nt(left, right):
    return lax.dot_general(left, right, (((1,), (1,)), ((), ())), preferred_element_type=f32)


def dot_nn(left, right):
    return lax.dot_general(left, right, (((1,), (0,)), ((), ())), preferred_element_type=f32)


def fold8(block):
    total = block[0:8]
    for k in range(8, block.shape[0], 8):
        total = total + block[k : k + 8]
    return total


def kernel(
    view1, view2, in1, in2, scale_ref,
    loss_ref, w1_ref, w2_ref,
    V1, V2, D1, D2, X1, X2, P1, P2, PT,
    zs, zr, cs, cr, xs, xr, ys, yr, U1, U2,
    C, G, GH, GL, M1, M2, A1, R1, A2, R2, AL, RL,
    ssem, rsem, lsem,
):
    R = view1.shape[0]
    B = V1.shape[0]
    T = V1.shape[1]
    dp = lax.axis_index("dp")
    ft = lax.axis_index("feat")
    c = lax.rem(dp, 2)
    x = lax.rem(lax.div(dp, 2), NX)
    yl = lax.div(dp, 2 * NX)
    yh = lax.rem(ft, 2)
    z = lax.div(ft, 2)

    def dpi(r, dx, other=0):
        y_ = yl if r == 0 else 1 - yl
        c_ = 1 - c if other else c
        return (y_ * NX + lax.rem(x + (dx % NX), NX)) * 2 + c_

    turn = 1 - 2 * c

    def fti(r, dz):
        y_ = yh if r == 0 else 1 - yh
        return lax.rem(z + NZ + dz * turn, NZ) * 2 + y_

    def rows(i):
        return pl.ds(pl.multiple_of(i * R, 16), R)

    def at(buf, i, u=None):
        if u is None:
            return buf.at[rows(i)]
        return buf.at[pl.ds(pl.multiple_of(i * R + PIECES[u][0], 16), PIECES[u][1])]

    def part(buf, slot, u):
        return buf.at[slot, pl.ds(*PIECES[u])]

    to_core = {"dp": dpi(0, 0, 1), "feat": ft}
    to_yl = {"dp": dpi(1, 0), "feat": ft}
    to_yh = {"dp": dp, "feat": fti(1, 0)}
    to = {
        "xp": {"dp": dpi(0, 1), "feat": ft},
        "xm": {"dp": dpi(0, -1), "feat": ft},
        "p": {"dp": dp, "feat": fti(0, 1)},
        "m": {"dp": dp, "feat": fti(0, -1)},
    }
    xa = x + 1 - 2 * lax.rem(x, 2)
    xb = NX - 1 - x
    za = z + 1 - 2 * lax.rem(z, 2)
    zb = z + 2 - 4 * lax.rem(lax.div(z, 2), 2)
    dp_steps = [
        to_core,
        to_yl,
        {"dp": (yl * NX + xa) * 2 + c, "feat": ft},
        {"dp": (yl * NX + xb) * 2 + c, "feat": ft},
    ]
    to_zb = {"dp": dp, "feat": zb * 2 + yh}
    to_zc = {"dp": dp, "feat": fti(0, 4)}
    feat_steps = [to_yh, {"dp": dp, "feat": za * 2 + yh}, to_zb, to_zc]

    peers = [to_core, to_yl, to_yh, to["xp"], to["xm"], to["p"], to["m"], to_zb, to_zc]
    barrier = pltpu.get_barrier_semaphore()
    for peer in peers:
        pl.semaphore_signal(barrier, inc=1, device_id=peer, device_id_type=MESH)
    local = [
        pltpu.make_async_copy(view1, at(V1, dp), lsem.at[0]),
        pltpu.make_async_copy(view2, at(V2, ft), lsem.at[1]),
        pltpu.make_async_copy(in1, X1, lsem.at[2]),
        pltpu.make_async_copy(in2, X2, lsem.at[3]),
    ]
    for copy in local:
        copy.start()
    pl.semaphore_wait(barrier, len(peers))

    names = {}

    def index(name):
        if name[0] in ("g", "d"):
            name = ("gather",) + name[1:]
        return names.setdefault(name, len(names))

    def group(name):
        if name[0] in ("g", "d"):
            return 0 if name[1] in ("yl", "xp", "xm", "c") else 1
        if name[0] == "s":
            return 2 if isinstance(name[1], tuple) else 3
        return ("a1", "a2", "al").index(name[0]) + 4

    def send(name, src, dst, dev):
        pltpu.make_async_remote_copy(
            src_ref=src, dst_ref=dst, send_sem=ssem.at[group(name)], recv_sem=rsem.at[index(name)],
            device_id=dev, device_id_type=MESH,
        ).start()

    def recv(name, dst):
        pltpu.make_async_remote_copy(
            src_ref=dst, dst_ref=dst, send_sem=ssem.at[0], recv_sem=rsem.at[index(name)],
            device_id=to_core, device_id_type=MESH,
        ).wait_recv()

    def drain(which, ref):
        pltpu.make_async_remote_copy(
            src_ref=ref, dst_ref=ref, send_sem=ssem.at[which], recv_sem=rsem.at[0],
            device_id=to_core, device_id_type=MESH,
        ).wait_send()

    def start_a(tag, A, src):
        own = at(A, dp)
        send((tag, "yl"), src, own, to_yl)
        send((tag, "xp", 0, 1), src, own, to["xp"])
        send((tag, "xm", 0, 1), src, own, to["xm"])
        send((tag, "c"), src, own, to_core)

    def start_b(tag, Bb, src, u):
        for d in ("p", "m"):
            send((tag, d, 0, 1, u), src.at[pl.ds(*PIECES[u])], at(Bb, ft, u), to[d])

    def ev_yl(tag, A):
        i = dpi(1, 0)
        recv((tag, "yl"), at(A, i))
        send((tag, "xp", 1, 1), at(A, i), at(A, i), to["xp"])
        send((tag, "xm", 1, 1), at(A, i), at(A, i), to["xm"])
        send((tag, "c"), at(A, i), at(A, i), to_core)
        return i

    def z_name(tag, d, r, h, u):
        return (tag, d, r, h) if (d, r, h) in FINAL else (tag, d, r, h, u)

    def ev_z(tag, Bb, d, r, h, u):
        i = fti(r, -h if d == "p" else h)
        if (d, r, h) in FINAL:
            if u == 0:
                recv((tag, d, r, h), at(Bb, i))
            return i
        piece = at(Bb, i, u)
        recv((tag, d, r, h, u), piece)
        if r == 0 and (d, h) in (("m", 1), ("p", 2)):
            send((tag, "y", d, h, u), piece, piece, to_yh)
        if h < (4 if d == "p" else 3):
            send(z_name(tag, d, r, h + 1, u), piece, piece, to[d])
        return i

    def ev_y(tag, Bb, d, h, u):
        i = fti(1, -h if d == "p" else h)
        piece = at(Bb, i, u)
        recv((tag, "y", d, h, u), piece)
        send(z_name(tag, d, 1, h + 1, u), piece, piece, to[d])
        return i

    def ev_x(tag, A, d, r, h):
        dx = (-SIGN[d] * h) % NX
        i = dpi(r, dx)
        recv((tag, d, r, h), at(A, i))
        if h < KX[d, r]:
            send((tag, d, r, h + 1), at(A, i), at(A, i), to[d])
        send((tag, "c"), at(A, i), at(A, i), to_core)
        return i

    def late_send(tag, Bb, n):
        block = at(Bb, fti(0, -n))
        send((tag, "y"), block, block, to_yh)

    def gather(tag, A, Bb, hook_a, hook_b, after):
        last = len(PIECES) - 1
        for n, steps in enumerate(ORDER):
            work = []
            for kind, *args in steps:
                if kind == "z" or kind == "y":
                    i = (ev_z if kind == "z" else ev_y)(tag, Bb, *args)
                    if n == len(ORDER) - 1:
                        hook_b(i, args[-1])
                    elif args[-1] == last:
                        work.append((hook_b, i))
                elif kind == "ls":
                    late_send(tag, Bb, *args)
                elif kind == "lr":
                    recv((tag, "y"), Bb.at[pl.ds(0, 2 * R)])
                    work += [(hook_b, fti(1, 0)), (hook_b, fti(1, -1))]
                elif kind == "yl":
                    work.append((hook_a, ev_yl(tag, A)))
                elif kind == "x":
                    work.append((hook_a, ev_x(tag, A, *args)))
                else:
                    recv((tag, "c"), A.at[pl.ds(0, len(CORDER) * R)])
                    work += [(hook_a, dpi(r, dx, 1)) for r, dx in CORDER]
            for hook, i in work:
                hook(i)
            if n in after:
                after[n]()

    CH = 48

    def span(u):
        return (0, R) if u is None else PIECES[u]

    def moments(V, M, i, u=None):
        start, count = span(u)
        base = i * R + start
        step = next(n for n in (48, 32, 16) if count % n == 0)

        def body(k, carry):
            s, q = carry
            v = V[pl.ds(pl.multiple_of(base + k * step, 16), step), :].astype(f32)
            return s + fold8(v), q + fold8(v * v)

        s, q = lax.fori_loop(0, count // step, body, (M[0:8, :], M[8:16, :]))
        M[0:8, :] = s
        M[8:16, :] = q

    def piece_rows(i, u):
        start, count = span(u)
        return pl.ds(pl.multiple_of(i * R + start, 16), count)

    def statistics(M):
        average = jnp.sum(M[0:8, :], axis=0, keepdims=True) / B
        spread = jnp.sum(M[8:16, :], axis=0, keepdims=True) / B - average * average
        M[16:24, :] = jnp.broadcast_to(lax.rsqrt(spread + epsilon), (8, T))
        M[32:40, :] = jnp.broadcast_to(average, (8, T))

    def normalize(V, M):
        average = M[32:33, :]
        inv = M[16:17, :]

        def body(k, total):
            at_ = pl.ds(pl.multiple_of(k * CH, 16), CH)
            n = ((V[at_, :].astype(f32) - average) * inv).astype(bf16)
            V[at_, :] = n
            return total + fold8(n.astype(f32))

        total = lax.fori_loop(0, B // CH, body, jnp.zeros((8, T), f32))
        M[24:32, :] = jnp.broadcast_to(jnp.sum(total, axis=0, keepdims=True), (8, T))

    M1[...] = jnp.zeros_like(M1)
    M2[...] = jnp.zeros_like(M2)
    for u in range(NP):
        start_b("g", V2, view2, u)
    start_a("g", V1, view1)
    local[0].wait()
    local[1].wait()
    moments(V1, M1, dp)
    moments(V2, M2, ft)

    ready = []
    waiting = [ft]

    def corr(i, u=None):
        at_ = piece_rows(i, u)
        C[...] += dot_tn(V1[at_, :], V2[at_, :])

    def work_two(i, u=None):
        moments(V2, M2, i, u)
        if ready:
            corr(i, u)
        else:
            waiting.append(i)

    def some(count):
        for _ in range(min(count, len(waiting))):
            corr(waiting.pop(0))

    def first_whole():
        drain(0, V1.at[pl.ds(0, 15 * R)])
        statistics(M1)
        normalize(V1, M1)
        C[...] = jnp.zeros_like(C)
        ready.append(True)
        some(3)

    after = {WHOLE: first_whole, WHOLE + 1: lambda: some(3), WHOLE + 2: lambda: some(5), WHOLE + 3: lambda: some(20)}
    gather("g", V1, V2, lambda i: moments(V1, M1, i), work_two, after)
    statistics(M2)

    KC = 768
    lane_row = lax.broadcasted_iota(jnp.int32, (16, T), 0)

    def split(value):
        high = value.astype(bf16).astype(f32)
        return high, value - high

    s_high, s_low = split(jnp.concatenate([M1[24:32, :], M1[24:32, :]], axis=0))
    a_high, a_low = split(jnp.concatenate([M2[32:40, :], M2[32:40, :]], axis=0))
    left = jnp.where(lane_row < 2, s_high, jnp.where(lane_row < 4, s_low, 0.0)).astype(bf16)
    right = jnp.where(lane_row % 2 == 0, a_high, a_low).astype(bf16)
    C[...] -= dot_tn(left, right)

    CG = 32
    scale = scale_ref[0]
    inv_two = M2[16:17, :] / B
    row0 = ft * T
    col0 = dp * T

    def tile(k):
        at_ = pl.ds(pl.multiple_of(k * CG, CG), CG)
        corr_ = C[at_, :] * inv_two
        row_ids = row0 + k * CG + lax.broadcasted_iota(jnp.int32, (CG, T), 0)
        col_ids = col0 + lax.broadcasted_iota(jnp.int32, (CG, T), 1)
        return at_, corr_, row_ids == col_ids, 1.0 - corr_

    def grad(k, carry):
        at_, corr_, on, miss = tile(k)
        G[at_, :] = (jnp.where(on, -2.0 * miss, 2.0 * off_weight * corr_) * scale).astype(bf16)
        return carry

    lax.fori_loop(0, T // CG, grad, 0)

    def terms(k, loss):
        at_, corr_, on, miss = tile(k)
        prod = G[at_, :].astype(f32) * corr_
        high = prod.astype(bf16)
        GH[at_, :] = high
        GL[at_, :] = (prod - high.astype(f32)).astype(bf16)
        return loss + fold8(jnp.where(on, miss * miss, off_weight * corr_ * corr_))

    DC = 16

    def delta(U, V, M, A, D, i, start, count):
        stats = A[4]
        first = jnp.concatenate([stats[k : k + 1] for k in range(4)], axis=1) / B
        second = jnp.concatenate([stats[k : k + 1] for k in range(4, 8)], axis=1) / B
        inv = M[16:17, :]

        def body(k, carry):
            off = pl.multiple_of(start + k * DC, 16)
            at_ = pl.ds(pl.multiple_of(i * R + start + k * DC, 16), DC)
            own = V[at_, :].astype(f32)
            D[at_, :] = (inv * (U[pl.ds(off, DC), :] / B - first - own * second)).astype(bf16)
            return carry

        lax.fori_loop(0, count // DC, body, 0)

    def pair2(dz):
        at_ = pl.ds(pl.multiple_of(fti(0, dz) // 2 * (2 * R), 16), 2 * R)
        P2[at_, :] = dot_nn(V1[at_, :], G[...])

    def pair1(r, dx):
        PT[...] = dot_nt(V2[pl.ds(pl.multiple_of(dpi(r, dx) // 2 * (2 * R), 16), 2 * R), :], G[...])
        P1[CSLOT[r, dx]] = PT[rows(c), :]

    def p2(i, u):
        return P2[pl.ds(pl.multiple_of(i * R + PIECES[u][0], 16), PIECES[u][1]), :]

    def arrived(key, u):
        slot = ZSLOT[key]
        recv(("s", key, u), part(zr, slot, u))
        return part(zr, slot, u)[...].astype(f32)

    def zc(u, r, k, over_y=False, take=()):
        key = ("y", k) if over_y else (r, k)
        dev = to_yh if over_y else to["m"] if k > 0 else to["p"]
        val = p2(fti(r, -k), u)
        for source in take:
            val = val + arrived(source, u)
        part(zs, ZSLOT[key], u)[...] = val.astype(bf16)
        send(("s", key, u), part(zs, ZSLOT[key], u), part(zr, ZSLOT[key], u), dev)

    def z_end(u):
        val = p2(fti(0, 0), u)
        for source in ((0, 1), (0, -1), ("y", 0)):
            val = val + arrived(source, u)
        U2[pl.ds(*PIECES[u]), :] = val
        delta(U2, V2, M2, A2, D2, ft, *PIECES[u])
        start_b("d", D2, at(D2, ft), u)

    def far(u):
        if u == 0:
            pair2(-4)
        zc(u, 1, 4)
        if u == 0:
            pair2(3)
        zc(u, 1, -3)

    def far_own(u):
        zc(u, 0, 4)
        zc(u, 0, -3)

    def middle(u):
        if u == 0:
            pair2(-3)
            pair2(2)
        zc(u, 1, 3, take=[(1, 4)])
        zc(u, 1, -2, take=[(1, -3)])

    def middle_own(u):
        zc(u, 0, 3, take=[(0, 4)])
        zc(u, 0, -2, take=[(0, -3)])

    def cross(u):
        if u == 0:
            pair2(-2)
            pair2(1)
        zc(u, 1, 2, True, take=[(1, 3)])
        zc(u, 1, -1, True, take=[(1, -2)])

    def near(u):
        zc(u, 0, 2, take=[(0, 3), ("y", 2)])
        zc(u, 0, -1, take=[(0, -2), ("y", -1)])

    def nearest(u):
        zc(u, 0, 1, take=[(0, 2), ("y", 1)])

    def core_send(r, dx):
        pair1(r, dx)
        slot = CSLOT[r, dx]
        cs[slot] = PT[rows(1 - c), :].astype(bf16)
        send(("s", "c", slot >= 2), cs.at[slot], cr.at[slot], to_core)

    def both(r, dx):
        dx = dx % NX
        slot = CSLOT[r, dx]
        val = P1[slot]
        if slot == 0:
            recv(("s", "c", False), cr.at[pl.ds(0, 2)])
        if slot == 2:
            recv(("s", "c", True), cr.at[pl.ds(2, 6)])
        return val + cr[slot].astype(f32)

    def xc(d, r, s):
        val = both(r, SIGN[d] * (KX[d, r] - s))
        if s:
            prev = XSLOT[d, r, s - 1]
            recv(("s", d, r, s - 1), xr.at[prev])
            val = val + xr[prev].astype(f32)
        slot = XSLOT[d, r, s]
        xs[slot] = val.astype(bf16)
        send(("s", d, r, s), xs.at[slot], xr.at[slot], to[d])

    def x_end(r):
        val = both(r, 0)
        for d in ("xp", "xm"):
            last = KX[d, r] - 1
            slot = XSLOT[d, r, last]
            recv(("s", d, r, last), xr.at[slot])
            val = val + xr[slot].astype(f32)
        return val

    far(0)
    far(1)
    drain(1, V2.at[pl.ds(0, 15 * R)])
    normalize(V2, M2)
    pair2(-1)
    zc(0, 1, 1, True)
    zc(1, 1, 1, True)
    pair2(0)
    zc(0, 1, 0, True)
    zc(1, 1, 0, True)
    for r, dx in CORDER[0:4]:
        core_send(r, dx)
    middle(0)
    far_own(0)
    xc("xp", 0, 0)
    xc("xm", 1, 0)
    middle(1)
    for r, dx in CORDER[4:8]:
        core_send(r, dx)
    far_own(1)
    cross(0)
    xc("xp", 1, 0)
    xc("xm", 0, 0)
    cross(1)
    middle_own(0)
    def put(n):
        send(("a1", n), A1.at[n], R1.at[n], dp_steps[n])
        send(("a2", n), A2.at[n], R2.at[n], feat_steps[n])

    def take(n):
        recv(("a1", n), R1.at[n])
        recv(("a2", n), R2.at[n])
        A1[n + 1] = A1[n] + R1[n]
        A2[n + 1] = A2[n] + R2[n]

    loss = lax.fori_loop(0, T // CG, terms, jnp.zeros((8, T), f32))
    loss_tile = loss[:, 0:128]
    for k in range(128, T, 128):
        loss_tile = loss_tile + loss[:, k : k + 128]

    ones = jnp.ones((16, T), bf16)
    second1 = dot_nt(ones, GH[...]) + dot_nt(ones, GL[...])
    second2 = dot_nn(ones, GH[...]) + dot_nn(ones, GL[...])

    def split_rows(M):
        s = jnp.concatenate([M[24:32, :], M[24:32, :]], axis=0)
        high = s.astype(bf16).astype(f32)
        low = s - high
        return jnp.where(lane_row == 0, high, jnp.where(lane_row == 1, low, 0.0)).astype(bf16)

    first1 = jnp.sum(dot_nt(split_rows(M2), G[...]), axis=0, keepdims=True) / B
    first2 = jnp.sum(dot_nn(split_rows(M1), G[...]), axis=0, keepdims=True) / B

    for k in range(T // 128):
        lanes = slice(k * 128, k * 128 + 128)
        A1[0, k : k + 1, :] = first1[:, lanes]
        A1[0, 4 + k : 5 + k, :] = second1[0:1, lanes]
        A2[0, k : k + 1, :] = first2[:, lanes]
        A2[0, 4 + k : 5 + k, :] = second2[0:1, lanes]
    A1[0, 8:16, :] = loss_tile

    put(0)
    middle_own(1)
    xc("xp", 0, 1)
    xc("xm", 1, 1)
    take(0)
    put(1)
    near(0)
    near(1)
    take(1)
    put(2)
    ys[0] = x_end(1).astype(bf16)
    send(("s", "yl"), ys.at[0], yr.at[0], to_yl)
    take(2)
    put(3)

    nearest(0)
    take(3)
    nearest(1)
    z_end(0)
    val = x_end(0)
    recv(("s", "yl"), yr.at[0])
    U1[...] = val + yr[0].astype(f32)
    delta(U1, V1, M1, A1, D1, dp, 0, R)
    start_a("d", D1, at(D1, dp))
    z_end(1)
    AL[0] = A1[4, 8:16, :]

    def put_l(n):
        send(("al", n), AL.at[n], RL.at[n], feat_steps[n])

    def take_l(n):
        recv(("al", n), RL.at[n])
        AL[n + 1] = AL[n] + RL[n]

    put_l(0)
    take_l(0)
    put_l(1)

    local[2].wait()
    local[3].wait()

    def weight(w_ref, X, D, i, u=None, first=False):
        at_ = piece_rows(i, u)
        term = dot_tn(X[at_, :], D[at_, :])
        if first:
            w_ref[...] = term
        else:
            w_ref[...] += term

    def weights_one():
        w1_ref[...] = dot_tn(X1[0:KC, :], D1[0:KC, :])

        def body(k, carry):
            at_ = pl.ds(pl.multiple_of(k * KC, 16), KC)
            w1_ref[...] += dot_tn(X1[at_, :], D1[at_, :])
            return carry

        lax.fori_loop(1, B // KC, body, 0)

    def loss_step(n):
        take_l(n)
        if n < 3:
            put_l(n + 1)
        else:
            loss_ref[0] = jnp.sum(AL[4]) / F

    weight(w2_ref, X2, D2, ft, first=True)
    after = {0: lambda: loss_step(1), 2: lambda: loss_step(2), 4: lambda: loss_step(3), WHOLE: weights_one}
    gather("d", D1, D2, lambda i: None, lambda i, u=None: weight(w2_ref, X2, D2, i, u), after)
    drain(0, D1.at[pl.ds(0, 15 * R)])
    drain(1, D2.at[pl.ds(0, 15 * R)])
    drain(2, zs)
    drain(3, zs)
    drain(4, A1.at[pl.ds(0, 4)])
    drain(5, A2.at[pl.ds(0, 4)])
    drain(6, AL.at[pl.ds(0, 4)])
    assert len(names) == NSEM, len(names)


def per_device(view_one, view_two, inputs_one, inputs_two, loss_scale):
    R, T = view_one.shape
    B = inputs_one.shape[0]
    block = (R, T)
    anywhere = pl.BlockSpec(memory_space=pl.ANY)
    vmem = pl.BlockSpec(memory_space=pltpu.VMEM)
    smem = pl.BlockSpec(memory_space=pltpu.SMEM)
    V = pltpu.VMEM
    scratch = [
        V((B, T), bf16), V((B, T), bf16), V((B, T), bf16), V((B, T), bf16),
        V((B, T), bf16), V((B, T), bf16), V((len(CSLOT),) + block, f32), V((B, T), f32), V((2 * R, T), f32),
        V((len(ZSLOT),) + block, bf16), V((len(ZSLOT),) + block, bf16),
        V((len(CSLOT),) + block, bf16), V((len(CSLOT),) + block, bf16),
        V((len(XSLOT),) + block, bf16), V((len(XSLOT),) + block, bf16),
        V((1,) + block, bf16), V((1,) + block, bf16),
        V(block, f32), V(block, f32),
        V((T, T), f32), V((T, T), bf16), V((T, T), bf16), V((T, T), bf16),
        V((40, T), f32), V((40, T), f32),
        V((5, 16, 128), f32), V((4, 16, 128), f32),
        V((5, 8, 128), f32), V((4, 8, 128), f32),
        V((5, 8, 128), f32), V((4, 8, 128), f32),
        pltpu.SemaphoreType.DMA((7,)),
        pltpu.SemaphoreType.DMA((NSEM,)),
        pltpu.SemaphoreType.DMA((4,)),
    ]
    return pl.pallas_call(
        kernel,
        out_shape=(
            jax.ShapeDtypeStruct((1,), f32),
            V((T, T), f32),
            V((T, T), f32),
        ),
        in_specs=[anywhere] * 4 + [smem],
        out_specs=(smem, vmem, vmem),
        scratch_shapes=scratch,
        compiler_params=pltpu.CompilerParams(
            collective_id=0, has_side_effects=True, vmem_limit_bytes=59 * 1024 * 1024
        ),
        cost_estimate=pl.CostEstimate(
            flops=10 * B * T * T, bytes_accessed=4 * B * T + 8 * T * T, transcendentals=0
        ),
    )(view_one, view_two, inputs_one, inputs_two, loss_scale)


def solution(mesh):
    placed = (P("dp", "feat"), P("feat", "dp"), P(None, "dp"), P(None, "feat"), P())
    return jax.shard_map(
        per_device,
        mesh=mesh,
        in_specs=placed,
        out_specs=(P(), P("dp", "feat"), P("feat", "dp")),
        check_vma=False,
    )
```
